256 devices in a mesh: seq: 32 (over z, y), head: 8 (over x, core).
Axes of the slice: x: 4, y: 4, z: 8, core: 2. Of those that a mesh axis runs over, the one named last changes fastest.
Arguments:
- queries: bfloat16 [32768, 32, 128], P('seq', 'head'), may hold values from -0.59765625 to 0.59765625
- keys: bfloat16 [32768, 32, 128], P('seq', 'head'), may hold values from -6 to 6
- values: bfloat16 [32768, 32, 128], P('seq', 'head'), may hold values from -6 to 6
- log_decay: float32 [32768, 32], P('seq', 'head'), may hold values from -0.8 to 0, as said below
- level_weight: float32 [32768, 32, 10], P('seq', 'head'), may hold values from 0.1 to 2
- norm_gain: float32 [32, 128], P('head'), may hold values from 0.25 to 1.75
- out_weight: bfloat16 [4096, 4096], P('head'), may hold values from -0.09375 to 0.09375
Outputs:
- mixed: bfloat16 [32768, 4096], P(('seq', 'head'))
The draws below stay inside these ranges and needn't reach their ends.
Inputs may be any that keep to these rules, and one draw needn't show every extreme that they name: `log_decay`: negative logarithms of decay factors.
All inputs are finite; a program needn't handle non-finite values.
Results may differ from the reference program's by a relative error of at most 0.023.
Values may be sent and summed in bfloat16 or wider, within the bound.
No kernel may reach another device: no remote copies, remote signals or barrier semaphores. Data moves between devices by JAX's collectives and lax.ppermute only.
A program may use at most 128 MiB of HBM per device.

```python
import math
import jax
import jax.numpy as jnp
import numpy as np
from jax import lax

D = 4096
HEAD_TOTAL = 32
HD = 128
SPAN = 64
TOK_DEV = 1024
LEVELS = 10
TOKEN_TOTAL = 32768
N_HEAD = 8


def decay_law(key, fast_share):
    variety_random_key, quick_random_key, gradual_random_key, block_random_key, token_random_key, spike_random_key, forget_random_key = jax.random.split(key, 7)
    fast_heads = jax.random.uniform(variety_random_key, (HEAD_TOTAL,)) < fast_share
    fast_rate = jnp.exp(jax.random.uniform(quick_random_key, (HEAD_TOTAL,), minval=math.log(1.0 / 50.0), maxval=math.log(1.0 / 30.0)))
    slow_rate = math.log(10.0) / TOKEN_TOTAL * jax.random.uniform(gradual_random_key, (HEAD_TOTAL,), minval=0.1, maxval=0.5)
    decay_speed = jnp.where(fast_heads, fast_rate, slow_rate)
    block_multiplier = jnp.exp(jax.random.uniform(block_random_key, (TOKEN_TOTAL // TOK_DEV, HEAD_TOTAL), minval=math.log(0.5), maxval=math.log(2.0)))
    block_multiplier = jnp.repeat(block_multiplier, TOK_DEV, axis=0)
    token_multiplier = jax.random.uniform(token_random_key, (TOKEN_TOTAL, HEAD_TOTAL), minval=0.5, maxval=1.5)
    decay_spikes = jax.random.uniform(spike_random_key, (TOKEN_TOTAL, HEAD_TOTAL)) < 2.0 / TOKEN_TOTAL
    forget_amount = jnp.log(jax.random.uniform(forget_random_key, (TOKEN_TOTAL, HEAD_TOTAL), minval=0.5, maxval=0.8))
    return -(decay_speed[None, :] * block_multiplier * token_multiplier) + jnp.where(decay_spikes, forget_amount, 0.0)


def draw_log_decay(key, part):
    key = jax.random.fold_in(key, 11)
    return decay_law(key, 0.5).astype(jnp.float32)


def steps_of(own_key, extent, shards, smallest, high):
    loudness, own = 1.0, jax.random.fold_in(own_key, 6)
    for dim, parts in shards:
        draws = jnp.exp(jax.random.uniform(jax.random.fold_in(own, dim), (parts,), jnp.float32, smallest / len(shards), high / len(shards)))
        loudness = loudness * jnp.repeat(draws, extent[dim] // parts).reshape([-1 if axis == dim else 1 for axis in range(len(extent))])
    return loudness


def noise(key, extent, deviation, bound, cuts=(), kind=jnp.bfloat16):
    entries = jax.random.normal(key, extent, jnp.float32) * deviation
    if len(cuts) > 0:
        entries = steps_of(key, extent, cuts, -0.22, 0.18) * entries
    return jnp.clip(entries, min=-bound, max=bound).astype(kind)


def setup_inputs(seed: int = 0) -> dict:
    key_of = jax.random.split(jax.random.key(seed), 8)
    return {
        "queries": noise(key_of[0], (TOKEN_TOTAL, HEAD_TOTAL, HD), 0.0884, 0.59765625, ((0, 32), (1, 8))),
        "keys": noise(key_of[1], (TOKEN_TOTAL, HEAD_TOTAL, HD), 1.0, 6.0, ((0, 32), (1, 8))),
        "values": noise(key_of[2], (TOKEN_TOTAL, HEAD_TOTAL, HD), 1.0, 6.0, ((0, 32), (1, 8))),
        "log_decay": draw_log_decay(jax.random.fold_in(key_of[7], 71), 0),
        "level_weight": jnp.clip(jnp.exp(math.log(2.0) - 2.9957323 * jax.random.uniform(key_of[4], (TOKEN_TOTAL, HEAD_TOTAL, LEVELS), jnp.float32) ** steps_of(key_of[4], (TOKEN_TOTAL, HEAD_TOTAL, LEVELS), ((0, 32), (1, 8)), -0.2, 0.2)), 0.1, 2.0),
        "norm_gain": jnp.clip(1.0 + 0.15 * jax.random.normal(key_of[5], (HEAD_TOTAL, HD), jnp.float32), 0.25, 1.75),
        "out_weight": noise(key_of[6], (HEAD_TOTAL * HD, D), (HEAD_TOTAL * HD) ** -0.5, 0.09375, ((0, 8),)),
    }


def span_terms(query_blocks, key_blocks, value_blocks, inner):
    size = inner.shape[1]
    scores = jnp.einsum('cthd,cshd->chts', query_blocks.astype(jnp.float32), key_blocks.astype(jnp.float32))
    leading = jnp.transpose(inner, (0, 2, 1))
    causal = np.tril(np.ones((size, size), dtype=bool))
    spread = jnp.where(causal, leading[:, :, :, None] - leading[:, :, None, :], 0.0)
    weight = jnp.where(causal, jnp.exp(spread), 0.0)
    probs = lax.optimization_barrier((scores * weight).astype(jnp.bfloat16))
    within = jnp.einsum('chts,cshe->cthe', probs.astype(jnp.float32), value_blocks.astype(jnp.float32))
    scaled = jnp.exp(inner[:, -1:, :] - inner)[:, :, :, None] * key_blocks.astype(jnp.float32)
    scaled = lax.optimization_barrier(scaled.astype(jnp.bfloat16))
    states = jnp.einsum('cshd,cshe->chde', scaled.astype(jnp.float32), value_blocks.astype(jnp.float32))
    return (within, states)

def level_terms(query_blocks, inner, states, totals, before, weights):
    count = states.shape[0]
    depth = count.bit_length() - 1
    output = jnp.zeros(query_blocks.shape, jnp.float32)
    blocks = states
    block_total = totals
    span_ids = np.arange(count)
    for level_now in range(1, depth + 1):
        shift_by = level_now - 1
        present = (span_ids >> shift_by & 1).astype(np.float32)
        source = np.maximum((span_ids >> shift_by) - 1, 0)
        middle = span_ids >> shift_by << shift_by
        picked = lax.optimization_barrier(blocks[source].astype(jnp.bfloat16))
        readout = jnp.einsum('cthd,chde->cthe', query_blocks.astype(jnp.float32), picked.astype(jnp.float32))
        factor = jnp.exp((before - before[middle])[:, None, :] + inner) * weights[:, :, :, level_now] * present[:, None, None]
        output = output + factor[:, :, :, None] * readout
        blocks = jnp.exp(block_total[1::2])[:, :, None, None] * blocks[0::2] + blocks[1::2]
        block_total = block_total[0::2] + block_total[1::2]
    return output

def reference(queries, keys, values, log_decay, level_weight, norm_gain, out_weight):
    count = TOKEN_TOTAL // SPAN

    def per_head(items):
        query_one, key_one, value_one, decay_one, weight_one = items
        shaped = (count, SPAN, 1, HD)
        query_blocks = query_one.reshape(shaped)
        key_blocks = key_one.reshape(shaped)
        value_blocks = value_one.reshape(shaped)
        weights = weight_one.reshape(count, SPAN, 1, LEVELS)
        inner = jnp.cumsum(decay_one.reshape(count, SPAN, 1), axis=1)
        totals = inner[:, -1, :]
        before = jnp.cumsum(totals, axis=0) - totals
        within, states = span_terms(query_blocks, key_blocks, value_blocks, inner)
        output = within * weights[:, :, :, 0:1]
        output = output + level_terms(query_blocks, inner, states, totals, before, weights)
        return output.reshape(TOKEN_TOTAL, HD)
    attention = lax.map(per_head, (jnp.transpose(queries, (1, 0, 2)), jnp.transpose(keys, (1, 0, 2)), jnp.transpose(values, (1, 0, 2)), jnp.transpose(log_decay, (1, 0)), jnp.transpose(level_weight, (1, 0, 2))))
    attention = jnp.transpose(attention, (1, 0, 2))
    mean_square = lax.optimization_barrier(jnp.mean(attention * attention, axis=-1, keepdims=True))
    normed = (attention * lax.rsqrt(mean_square + 1e-06) * norm_gain[None]).astype(jnp.bfloat16)
    normed = normed.reshape(TOKEN_TOTAL, HEAD_TOTAL * HD)
    group_width = HEAD_TOTAL // N_HEAD * HD
    summed = jnp.zeros((TOKEN_TOTAL, D), jnp.float32)
    for group_index in range(N_HEAD):
        lower_col = group_index * group_width
        partial_sum = jnp.dot(normed[:, lower_col:lower_col + group_width], out_weight[lower_col:lower_col + group_width], preferred_element_type=jnp.float32)
        partial_sum = lax.optimization_barrier(partial_sum.astype(jnp.bfloat16))
        summed = summed + partial_sum.astype(jnp.float32)
    return summed.astype(jnp.bfloat16)
```

```python
import functools
import jax
import jax.numpy as jnp
from jax import lax
from jax.experimental import pallas as pl
from jax.experimental.pallas import tpu as pltpu
from jax.sharding import PartitionSpec as P

SPAN = 64
HD = 128
BF = jnp.bfloat16
F32 = jnp.float32
VMEM_LIMIT = 48 * 1024 * 1024


def params(**kw):
    return pltpu.CompilerParams(vmem_limit_bytes=VMEM_LIMIT, **kw)


def dot(a, b):
    return jnp.dot(a, b, preferred_element_type=F32)


def lane_cumsum(x):
    lanes = lax.broadcasted_iota(jnp.int32, (x.shape[0], 128), 1)
    carry = jnp.zeros((x.shape[0], 1), F32)
    chunks = []
    for i in range(x.shape[1] // 128):
        c = x[:, i * 128 : (i + 1) * 128]
        step = 1
        while step < 128:
            c = c + jnp.where(lanes >= step, pltpu.roll(c, step, 1), 0.0)
            step *= 2
        chunks.append(c)
    out = []
    for c in chunks:
        out.append(c + carry)
        carry = carry + c[:, 127:128]
    return jnp.concatenate(out, axis=1)


def total_rows(total):
    high = total.astype(BF).astype(F32)
    mid = (total - high).astype(BF).astype(F32)
    low = total - high - mid
    rows = jnp.concatenate([high, mid, low, jnp.zeros_like(low)], axis=0)
    return rows.astype(BF)


def summary_kernel(ld_ref, k_ref, v_ref, state_ref, pay_ref, cum_ref, tot_ref, w_ref):
    h = pl.program_id(0)
    heads = ld_ref.shape[0]

    @pl.when(h == 0)
    def _():
        cum = lane_cumsum(ld_ref[...])
        total = cum[:, -1:]
        cum_ref[...] = cum
        w_ref[...] = jnp.exp(total - cum)
        wide = jnp.broadcast_to(total, (heads, 128))
        tot_ref[...] = wide
        pay_ref[heads * HD :, :] = total_rows(wide)

    row = w_ref[pl.ds(h, 1), :]
    vt = (v_ref[...].astype(F32).T * row).astype(BF)
    state = dot(vt, k_ref[...])
    state_ref[...] = state
    pay_ref[pl.ds(pl.multiple_of(h * HD, HD), HD), :] = state.astype(BF)


def summary(ld, k, v):
    heads, rows = ld.shape
    full = lambda *shape: pl.BlockSpec(shape, lambda h: (0,) * len(shape))
    return pl.pallas_call(
        summary_kernel,
        grid=(heads,),
        in_specs=[
            full(heads, rows),
            pl.BlockSpec((rows, HD), lambda h: (0, h)),
            pl.BlockSpec((rows, HD), lambda h: (0, h)),
        ],
        out_specs=[
            pl.BlockSpec((HD, HD), lambda h: (h, 0)),
            full(heads * HD + 16, 128),
            full(heads, rows),
            full(heads, 128),
        ],
        out_shape=[
            jax.ShapeDtypeStruct((heads * HD, HD), F32),
            jax.ShapeDtypeStruct((heads * HD + 16, 128), BF),
            jax.ShapeDtypeStruct((heads, rows), F32),
            jax.ShapeDtypeStruct((heads, 128), F32),
        ],
        scratch_shapes=[pltpu.VMEM((heads, rows), F32)],
        compiler_params=params(),
        name="summary",
        cost_estimate=pl.CostEstimate(flops=140_000_000, bytes_accessed=3_000_000, transcendentals=4096),
    )(ld, k, v)


def merge_kernel(pos_ref, recv_ref, state_ref, tot_ref, off_ref, state_out, pay_out, tot_out, off_out, *, bit):
    heads = tot_ref.shape[0]
    right = ((pos_ref[0] >> bit) & 1).astype(F32)
    rows = recv_ref[heads * HD :, :].astype(F32)
    there = rows[:heads] + rows[heads : 2 * heads] + rows[2 * heads : 3 * heads]
    here = tot_ref[...]
    total = here + there
    tot_out[...] = total
    off_out[...] = off_ref[...] + right * there
    pay_out[heads * HD :, :] = total_rows(total)
    keep = right + (1.0 - right) * jnp.exp(there)
    take = (1.0 - right) + right * jnp.exp(here)
    for h in range(heads):
        block = pl.ds(h * HD, HD)
        state = state_ref[block, :] * keep[h : h + 1] + recv_ref[block, :].astype(F32) * take[h : h + 1]
        state_out[block, :] = state
        pay_out[block, :] = state.astype(BF)


def merge(pos, recv, state, tot, off, bit):
    vm = pl.BlockSpec(memory_space=pltpu.VMEM)
    return pl.pallas_call(
        functools.partial(merge_kernel, bit=bit),
        in_specs=[pl.BlockSpec(memory_space=pltpu.SMEM), vm, vm, vm, vm],
        out_specs=[vm, vm, vm, vm],
        out_shape=[
            jax.ShapeDtypeStruct(state.shape, F32),
            jax.ShapeDtypeStruct(recv.shape, BF),
            jax.ShapeDtypeStruct(tot.shape, F32),
            jax.ShapeDtypeStruct(off.shape, F32),
        ],
        compiler_params=params(),
        name=f"merge{bit}",
        cost_estimate=pl.CostEstimate(flops=200_000, bytes_accessed=800_000, transcendentals=1024),
    )(pos, recv, state, tot, off)


def local_kernel(q_ref, k_ref, v_ref, cum_ref, lw_ref, acc_ref, qt_ref, *, head):
    rows = q_ref.shape[0]
    pair = 2 * SPAN
    qt = q_ref[...].astype(F32).T.astype(BF)
    qt_ref[...] = qt
    vt = v_ref[...].astype(F32).T
    cum = cum_ref[head : head + 1, :]
    weight = lambda level: lw_ref[level, head : head + 1, :]
    s_pos = lax.broadcasted_iota(jnp.int32, (pair, pair), 0)
    t_pos = lax.broadcasted_iota(jnp.int32, (pair, pair), 1)
    same = jnp.logical_and(s_pos <= t_pos, (s_pos >= SPAN) == (t_pos >= SPAN))
    cross = jnp.logical_and(s_pos < SPAN, t_pos >= SPAN)
    for i in range(rows // pair):
        at = slice(i * pair, (i + 1) * pair)
        middle = cum[:, i * pair + SPAN - 1 : i * pair + SPAN]
        grow = jnp.exp(cum[:, at] - middle)
        scores = dot(k_ref[at, :], qt[:, at])
        probs = scores * jnp.where(same, weight(0)[:, at], jnp.where(cross, weight(1)[:, at], 0.0))
        held = (vt[:, at] * jnp.exp(middle - cum[:, at])).astype(BF)
        acc_ref[:, at] = dot(held, probs.astype(BF)) * grow
    level, half = 2, pair
    while half < rows:
        for i in range(rows // (2 * half)):
            left = slice(2 * i * half, (2 * i + 1) * half)
            right = slice((2 * i + 1) * half, (2 * i + 2) * half)
            end = cum[:, left.stop - 1 : left.stop]
            held = (vt[:, left] * jnp.exp(end - cum[:, left])).astype(BF)
            bucket = dot(held, k_ref[left, :]).astype(BF)
            factor = weight(level)[:, right] * jnp.exp(cum[:, right] - end)
            acc_ref[:, right] += dot(bucket, qt[:, right]) * factor
        level, half = level + 1, half * 2


def local(q, k, v, cum, lw, head):
    rows = q.shape[0]
    col = pl.BlockSpec((rows, HD), lambda i: (0, head))
    return pl.pallas_call(
        functools.partial(local_kernel, head=head),
        grid=(1,),
        in_specs=[
            col,
            col,
            col,
            pl.BlockSpec(cum.shape, lambda i: (0, 0)),
            pl.BlockSpec(lw.shape, lambda i: (0, 0, 0)),
        ],
        out_specs=[pl.BlockSpec((HD, rows), lambda i: (0, 0))] * 2,
        out_shape=[jax.ShapeDtypeStruct((HD, rows), F32), jax.ShapeDtypeStruct((HD, rows), BF)],
        compiler_params=params(),
        name=f"local{head}",
        cost_estimate=pl.CostEstimate(flops=2_000_000_000, bytes_accessed=3_000_000, transcendentals=16384),
    )(q, k, v, cum, lw)


def far_term(pos_ref, recv_ref, off, qt, cum, lw_ref, head, bit, base):
    flag = ((pos_ref[0] >> bit) & 1).astype(F32)
    factor = lw_ref[base + bit, head : head + 1, :] * jnp.exp(off[head : head + 1, :1] + cum) * flag
    return dot(recv_ref[head * HD : (head + 1) * HD, :], qt) * factor


def far_kernel(pos_ref, *refs, heads, bits, base):
    accs, qts = refs[:heads], refs[heads : 2 * heads]
    recvs, offs = refs[2 * heads : 2 * heads + bits], refs[2 * heads + bits : 2 * heads + 2 * bits]
    cum_ref, lw_ref, out_ref = refs[2 * heads + 2 * bits :]
    for h in range(heads):
        acc = accs[h][...]
        qt = qts[h][...]
        cum = cum_ref[h : h + 1, :]
        for b in range(bits):
            acc = acc + far_term(pos_ref, recvs[b], offs[b][...], qt, cum, lw_ref, h, b, base)
        out_ref[h * HD : (h + 1) * HD, :] = acc


def far(pos, accs, qts, recvs, offs, cum, lw, base):
    heads, rows, bits = len(accs), cum.shape[1], len(recvs)
    width = min(256, rows)
    chunk = lambda *lead: pl.BlockSpec((*lead, width), lambda i: (0,) * len(lead) + (i,))
    whole = lambda a: pl.BlockSpec(a.shape, lambda i: (0,) * a.ndim)
    return pl.pallas_call(
        functools.partial(far_kernel, heads=heads, bits=bits, base=base),
        grid=(rows // width,),
        in_specs=[pl.BlockSpec(memory_space=pltpu.SMEM)]
        + [chunk(HD)] * (2 * heads)
        + [whole(a) for a in recvs]
        + [whole(a) for a in offs]
        + [chunk(heads), chunk(lw.shape[0], heads)],
        out_specs=chunk(heads * HD),
        out_shape=jax.ShapeDtypeStruct((heads * HD, rows), F32),
        compiler_params=params(),
        name="far",
        cost_estimate=pl.CostEstimate(flops=2_000_000_000, bytes_accessed=6_000_000, transcendentals=16384),
    )(pos, *accs, *qts, *recvs, *offs, cum, lw)


def norm_kernel(pick_ref, *refs, heads, bit, base):
    acc_ref, qts = refs[0], refs[1 : 1 + heads]
    recv_ref, off_ref, cum_ref, lw_ref, gain_ref, mine_ref, other_ref, tile_ref = refs[1 + heads :]
    flag = ((pick_ref[0] >> bit) & 1).astype(F32)
    core = pick_ref[1]
    for h in range(heads):
        at = slice(h * HD, (h + 1) * HD)
        factor = lw_ref[base + bit, h : h + 1, :] * jnp.exp(off_ref[h : h + 1, :1] + cum_ref[h : h + 1, :]) * flag
        att = acc_ref[at, :] + dot(recv_ref[at, :], qts[h][...]) * factor
        mean = jnp.mean(att * att, axis=0, keepdims=True)
        normed = (att * lax.rsqrt(mean + 1e-6)).T * gain_ref[h : h + 1, :]
        tile_ref[:, at] = normed.astype(BF)
    size = mine_ref.shape[0]
    mine_ref[...] = tile_ref[pl.ds(pl.multiple_of(core * size, size), size), :]
    other_ref[...] = tile_ref[pl.ds(pl.multiple_of((1 - core) * size, size), size), :]


def norm(pick, acc, qts, recv, off, cum, lw, gain, bit, base, slots):
    heads, rows = cum.shape
    width = rows // slots
    half = width // 2
    chunk = lambda *lead: pl.BlockSpec((*lead, width), lambda i, p: (0,) * len(lead) + (p[2 + i],))
    whole = lambda a: pl.BlockSpec(a.shape, lambda i, p: (0,) * a.ndim)
    return pl.pallas_call(
        functools.partial(norm_kernel, heads=heads, bit=bit, base=base),
        grid_spec=pltpu.PrefetchScalarGridSpec(
            num_scalar_prefetch=1,
            grid=(slots,),
            in_specs=[chunk(heads * HD)]
            + [chunk(HD)] * heads
            + [whole(recv), whole(off), chunk(heads), chunk(lw.shape[0], heads), whole(gain)],
            out_specs=[pl.BlockSpec((half, heads * HD), lambda i, p: (i, 0))] * 2,
            scratch_shapes=[pltpu.VMEM((width, heads * HD), BF)],
        ),
        out_shape=[jax.ShapeDtypeStruct((slots * half, heads * HD), BF)] * 2,
        compiler_params=params(),
        name="norm",
        cost_estimate=pl.CostEstimate(flops=300_000_000, bytes_accessed=5_000_000, transcendentals=8192),
    )(pick, acc, *qts, recv, off, cum, lw, gain)


def project_kernel(a_ref, b_ref, wa_ref, wb_ref, *refs):
    out_ref = refs[-1]
    total = dot(a_ref[...], wa_ref[...]) + dot(b_ref[...], wb_ref[...])
    for add in refs[:-1]:
        total = total + add[...].astype(F32)
    out_ref[...] = total.astype(out_ref.dtype)


def project(a, b, wa, wb, slot, rows, col0, cols, adds=(), out=BF, tile=512):
    depth = wa.shape[0]
    tiles = cols // tile
    first = col0 // tile
    left = pl.BlockSpec((rows, depth), lambda j: (slot, 0))
    weight = pl.BlockSpec((depth, tile), lambda j: (0, first + j))
    result = pl.BlockSpec((rows, tile), lambda j: (0, j))
    return pl.pallas_call(
        project_kernel,
        grid=(tiles,),
        in_specs=[left, left, weight, weight] + [result] * len(adds),
        out_specs=result,
        out_shape=jax.ShapeDtypeStruct((rows, cols), out),
        compiler_params=params(),
        name=f"project{slot}",
        cost_estimate=pl.CostEstimate(
            flops=4 * rows * depth * cols, bytes_accessed=4 * depth * cols, transcendentals=0
        ),
    )(a, b, wa, wb, *adds)


def finish_kernel(own_ref, lo1, lo2, hi1, hi2, out_ref):
    half = lo1.shape[1]
    out_ref[:, :half] = (own_ref[:, :half] + lo1[...].astype(F32) + lo2[...].astype(F32)).astype(BF)
    out_ref[:, half:] = (own_ref[:, half:] + hi1[...].astype(F32) + hi2[...].astype(F32)).astype(BF)


def finish(own, lo1, lo2, hi1, hi2):
    vm = pl.BlockSpec(memory_space=pltpu.VMEM)
    return pl.pallas_call(
        finish_kernel,
        in_specs=[vm] * 5,
        out_specs=vm,
        out_shape=jax.ShapeDtypeStruct(own.shape, BF),
        compiler_params=params(),
        name="finish",
        cost_estimate=pl.CostEstimate(flops=2_000_000, bytes_accessed=5_000_000, transcendentals=0),
    )(own, lo1, lo2, hi1, hi2)


def body(queries, keys, values, log_decay, level_weight, norm_gain, out_weight):
    rows, heads, _ = queries.shape
    seq_size, head_size = lax.axis_size("seq"), lax.axis_size("head")
    bits = seq_size.bit_length() - 1
    base = (rows // SPAN).bit_length()
    ring = head_size // 2
    pos = lax.axis_index("seq").astype(jnp.int32)
    lane = lax.axis_index("head").astype(jnp.int32)
    x, core = lane // 2, lane % 2
    pos1 = pos[None]
    pick = jnp.stack([pos, core] + [(x + d) % ring for d in (2, 1, 3, 0)])
    swap = [(i, i ^ 1) for i in range(head_size)]
    up = [(i, (i + 2) % head_size) for i in range(head_size)]
    down = [(i, (i - 2) % head_size) for i in range(head_size)]

    w_other = lax.ppermute(out_weight, "head", swap)
    k2 = keys.reshape(rows, heads * HD)
    v2 = values.reshape(rows, heads * HD)
    q2 = queries.reshape(rows, heads * HD)
    ld = jnp.transpose(log_decay, (1, 0))
    lw = jnp.transpose(level_weight, (2, 1, 0))

    state, pay, cum, tot = summary(ld, k2, v2)
    off = jnp.zeros((heads, 128), F32)
    recvs, offs, accs, qts = [], [], [], []
    for b in range(bits):
        pairs = [(i, i ^ (1 << b)) for i in range(seq_size)]
        if b == bits - 1:
            pairs = [(i, j) for i, j in pairs if i < j]
        recv = lax.ppermute(pay, "seq", pairs)
        recvs.append(recv)
        offs.append(off)
        if b < heads:
            acc, qt = local(q2, k2, v2, cum, lw, b)
            accs.append(acc)
            qts.append(qt)
        if b < bits - 1:
            state, pay, tot, off = merge(pos1, recv, state, tot, off, b)
    acc = far(pos1, accs, qts, recvs[:-1], offs[:-1], cum, lw, base)
    mine, other = norm(pick, acc, qts, recvs[-1], offs[-1], cum, lw, norm_gain, bits - 1, base, ring)
    theirs = lax.ppermute(other, "head", swap)

    depth = out_weight.shape[1]
    half = depth // 2
    part = mine.shape[0] // ring
    proj = functools.partial(project, mine, theirs, out_weight, w_other)
    a_lo = proj(0, part, 0, half)
    from_low = lax.ppermute(a_lo, "head", up)
    a_hi = proj(0, part, half, half)
    from_high = lax.ppermute(a_hi, "head", down)
    p_hi = proj(1, part, half, half)
    hi1 = lax.ppermute(p_hi, "head", up)
    m_lo = proj(2, part, 0, half)
    lo1 = lax.ppermute(m_lo, "head", down)
    own = proj(3, part, 0, depth, out=F32)
    p_lo = proj(1, part, 0, half, adds=(from_low,))
    lo2 = lax.ppermute(p_lo, "head", up)
    m_hi = proj(2, part, half, half, adds=(from_high,))
    hi2 = lax.ppermute(m_hi, "head", down)
    return finish(own, lo1, lo2, hi1, hi2)


def solution(mesh):
    return jax.shard_map(
        body,
        mesh=mesh,
        in_specs=(
            P("seq", "head", None),
            P("seq", "head", None),
            P("seq", "head", None),
            P("seq", "head"),
            P("seq", "head", None),
            P("head", None),
            P("head", None),
        ),
        out_specs=P(("seq", "head"), None),
        check_vma=False,
    )
```

```python
import functools
import jax
import jax.numpy as jnp
from jax import lax
from jax.experimental import pallas as pl
from jax.experimental.pallas import tpu as pltpu
from jax.sharding import PartitionSpec as P

SPAN = 64
HD = 128
BF = jnp.bfloat16
F32 = jnp.float32
VMEM_LIMIT = 16 * 1024 * 1024
VM = pl.BlockSpec(memory_space=pltpu.VMEM)
SM = pl.BlockSpec(memory_space=pltpu.SMEM)


def call(kernel, name, ins, outs, args, scratch=(), flops=0, moved=0, **kw):
    return pl.pallas_call(
        kernel,
        in_specs=ins,
        out_specs=[VM] * len(outs),
        out_shape=[jax.ShapeDtypeStruct(shape, dtype) for shape, dtype in outs],
        scratch_shapes=list(scratch),
        compiler_params=pltpu.CompilerParams(vmem_limit_bytes=VMEM_LIMIT),
        cost_estimate=pl.CostEstimate(flops=flops, bytes_accessed=moved, transcendentals=0),
        name=name,
        **kw,
    )(*args)


def dot(a, b):
    return jnp.dot(a, b, preferred_element_type=F32)


def lane_cumsum(x):
    lanes = lax.broadcasted_iota(jnp.int32, (x.shape[0], 128), 1)
    carry = jnp.zeros((x.shape[0], 1), F32)
    chunks = []
    for i in range(x.shape[1] // 128):
        c = x[:, i * 128 : (i + 1) * 128]
        step = 1
        while step < 128:
            c = c + jnp.where(lanes >= step, pltpu.roll(c, step, 1), 0.0)
            step *= 2
        chunks.append(c)
    out = []
    for c in chunks:
        out.append(c + carry)
        carry = carry + c[:, 127:128]
    return jnp.concatenate(out, axis=1)


def total_rows(total):
    high = total.astype(BF).astype(F32)
    mid = (total - high).astype(BF).astype(F32)
    low = total - high - mid
    rows = jnp.concatenate([high, mid, low, jnp.zeros_like(low)], axis=0)
    return rows.astype(BF)


def total_of(ref, heads):
    rows = ref[heads * HD :, :].astype(F32)
    return rows[:heads] + rows[heads : 2 * heads] + rows[2 * heads : 3 * heads]


def summary_kernel(ld_ref, k_ref, v_ref, pay_ref, cum_ref):
    heads = ld_ref.shape[0]
    cum = lane_cumsum(ld_ref[...])
    total = cum[:, -1:]
    cum_ref[...] = cum
    weight = jnp.exp(total - cum)
    pay_ref[heads * HD :, :] = total_rows(jnp.broadcast_to(total, (heads, 128)))
    for h in range(heads):
        at = slice(h * HD, (h + 1) * HD)
        vt = v_ref[:, at].astype(F32).T * weight[h : h + 1]
        pay_ref[at, :] = dot(vt.astype(BF), k_ref[:, at]).astype(BF)


def summary(ld, k, v):
    heads, rows = ld.shape
    return call(
        summary_kernel,
        "summary",
        [VM, VM, VM],
        [((heads * HD + 16, 128), BF), ((heads, rows), F32)],
        (ld, k, v),
        flops=140_000_000,
        moved=2_000_000,
    )


def merge_kernel(pos_ref, after_ref, recv_ref, self_ref, off_ref, pay_out, off_out, *, bit):
    heads = off_ref.shape[0]
    right = ((pos_ref[0] >> bit) & 1).astype(F32)
    there = total_of(recv_ref, heads)
    here = total_of(self_ref, heads)
    off_out[...] = off_ref[...] + right * there
    pay_out[heads * HD :, :] = total_rows(here + there)
    keep = right + (1.0 - right) * jnp.exp(there)
    take = (1.0 - right) + right * jnp.exp(here)
    for h in range(heads):
        block = slice(h * HD, (h + 1) * HD)
        state = self_ref[block, :].astype(F32) * keep[h : h + 1] + recv_ref[block, :].astype(F32) * take[h : h + 1]
        pay_out[block, :] = state.astype(BF)


def merge(pos, after, recv, pay, off, bit):
    return call(
        functools.partial(merge_kernel, bit=bit),
        f"merge{bit}",
        [SM, VM, VM, VM, VM],
        [(pay.shape, BF), (off.shape, F32)],
        (pos, after, recv, pay, off),
        flops=200_000,
        moved=600_000,
    )


def local_kernel(q_ref, k_ref, v_ref, cum_ref, lw_ref, acc_ref, qt_ref):
    heads, rows = cum_ref.shape
    pair = 2 * SPAN
    s_pos = lax.broadcasted_iota(jnp.int32, (pair, pair), 0)
    t_pos = lax.broadcasted_iota(jnp.int32, (pair, pair), 1)
    same = jnp.logical_and(s_pos <= t_pos, (s_pos >= SPAN) == (t_pos >= SPAN))
    cross = jnp.logical_and(s_pos < SPAN, t_pos >= SPAN)
    for h in range(heads):
        head = slice(h * HD, (h + 1) * HD)
        qt_ref[head, :] = q_ref[:, head].astype(F32).T.astype(BF)
        vt = v_ref[:, head].astype(F32).T
        cum = cum_ref[h : h + 1, :]
        weight = lambda level: lw_ref[level, h : h + 1, :]
        for i in range(rows // pair):
            at = slice(i * pair, (i + 1) * pair)
            middle = cum[:, i * pair + SPAN - 1 : i * pair + SPAN]
            grow = jnp.exp(cum[:, at] - middle)
            scores = dot(k_ref[at, head], qt_ref[head, at])
            probs = scores * jnp.where(same, weight(0)[:, at], jnp.where(cross, weight(1)[:, at], 0.0))
            held = (vt[:, at] * jnp.exp(middle - cum[:, at])).astype(BF)
            acc_ref[head, at] = dot(held, probs.astype(BF)) * grow
        level, half = 2, pair
        while half < rows:
            for i in range(rows // (2 * half)):
                left = slice(2 * i * half, (2 * i + 1) * half)
                right = slice((2 * i + 1) * half, (2 * i + 2) * half)
                end = cum[:, left.stop - 1 : left.stop]
                held = (vt[:, left] * jnp.exp(end - cum[:, left])).astype(BF)
                bucket = dot(held, k_ref[left, head]).astype(BF)
                factor = weight(level)[:, right] * jnp.exp(cum[:, right] - end)
                acc_ref[head, right] += dot(bucket, qt_ref[head, right]) * factor
            level, half = level + 1, half * 2


def local(q, k, v, cum, lw):
    heads, rows = cum.shape
    return call(
        local_kernel,
        "local",
        [VM] * 5,
        [((heads * HD, rows), F32), ((heads * HD, rows), BF)],
        (q, k, v, cum, lw),
        flops=2_000_000_000,
        moved=8_000_000,
    )


def far_factor(pos_ref, off_ref, cum, weight, head, bit):
    flag = ((pos_ref[0] >> bit) & 1).astype(F32)
    return weight * jnp.exp(off_ref[head : head + 1, :1] + cum) * flag


def far_kernel(pos_ref, acc_ref, qt_ref, recv_ref, off_ref, cum_ref, lw_ref, out_ref, *, bit, base):
    heads, rows = cum_ref.shape
    width = min(256, rows)
    for h in range(heads):
        head = slice(h * HD, (h + 1) * HD)
        for i in range(rows // width):
            at = slice(i * width, (i + 1) * width)
            factor = far_factor(pos_ref, off_ref, cum_ref[h : h + 1, at], lw_ref[base + bit, h : h + 1, at], h, bit)
            out_ref[head, at] = acc_ref[head, at] + dot(recv_ref[head, :], qt_ref[head, at]) * factor


def far(pos, acc, qt, recv, off, cum, lw, bit, base):
    return call(
        functools.partial(far_kernel, bit=bit, base=base),
        f"far{bit}",
        [SM] + [VM] * 6,
        [(acc.shape, F32)],
        (pos, acc, qt, recv, off, cum, lw),
        flops=300_000_000,
        moved=3_000_000,
        input_output_aliases={1: 0},
    )[0]


def norm_kernel(pick_ref, acc_ref, qt_ref, recv_ref, off_ref, cum_ref, lw_ref, gain_ref, near_ref, side_ref, own_ref, *, bit, base):
    heads = gain_ref.shape[0]
    core = pick_ref[1]
    size = own_ref.shape[0] // 2
    targets = (((near_ref, 0), (side_ref, 0)), ((near_ref, 1),), ((side_ref, 1),), ((own_ref, 0),))
    for i, outs in enumerate(targets):
        start = pick_ref[3 + i] * (2 * size)
        for part, offset in enumerate((core * size, (1 - core) * size)):
            at = pl.ds(pl.multiple_of(start + offset, size), size)
            for h in range(heads):
                head = slice(h * HD, (h + 1) * HD)
                factor = far_factor(pick_ref, off_ref, cum_ref[h : h + 1, at], lw_ref[base + bit, h : h + 1, at], h, bit)
                att = acc_ref[head, at] + dot(recv_ref[head, :], qt_ref[head, at]) * factor
                mean = jnp.mean(att * att, axis=0, keepdims=True)
                normed = ((att * lax.rsqrt(mean + 1e-6)).T * gain_ref[h : h + 1, :]).astype(BF)
                for out_ref, slot in outs:
                    first = (2 * slot + part) * size
                    out_ref[first : first + size, head] = normed


def norm(pick, acc, qt, recv, off, cum, lw, gain, bit, base, ring):
    heads, rows = cum.shape
    size = rows // ring
    return call(
        functools.partial(norm_kernel, bit=bit, base=base),
        "norm",
        [SM] + [VM] * 7,
        [((2 * size, heads * HD), BF)] * 2 + [((size, heads * HD), BF)],
        (pick, acc, qt, recv, off, cum, lw, gain),
        flops=400_000_000,
        moved=4_000_000,
    )


def start_kernel(a_ref, w_ref, out_ref, *, side, tile):
    rows, half = out_ref.shape
    for j in range(half // tile):
        own = slice(side * half + j * tile, side * half + (j + 1) * tile)
        out_ref[:, j * tile : (j + 1) * tile] = dot(a_ref[rows:, :], w_ref[:, own]).astype(BF)


def start(a, w, side, name, tile=512):
    shape = (a.shape[0] // 2, w.shape[1] // 2)
    kernel = functools.partial(start_kernel, side=side, tile=tile)
    return call(kernel, name, [VM, VM], [(shape, BF)], (a, w), flops=600_000_000, moved=3_000_000)[0]


def across(b_ref, rows, whole_ref, mine_ref, theirs_ref, side, col, parity):
    depth, share = whole_ref.shape[0], mine_ref.shape[0]
    second = b_ref[rows, pl.ds(pl.multiple_of(depth + parity * share, share), share)]
    third = b_ref[rows, pl.ds(pl.multiple_of(depth + (1 - parity) * share, share), share)]
    total = dot(b_ref[rows, :depth], whole_ref[:, col]) + dot(second, mine_ref[:, col])
    return total + dot(third, theirs_ref[side * share : (side + 1) * share, col])


def pass_kernel(pick_ref, begun_ref, b_ref, whole_ref, mine_ref, theirs_ref, kept_ref, sent_ref, *, side, tile):
    size, half = kept_ref.shape
    for j in range(half // tile):
        col = slice(j * tile, (j + 1) * tile)
        more = across(b_ref, slice(0, 2 * size), whole_ref, mine_ref, theirs_ref, side, col, pick_ref[2])
        total = begun_ref[:, col].astype(F32) + more
        kept_ref[:, col] = total[:size]
        sent_ref[:, col] = total[size:].astype(BF)


def pass_on(pick, begun, b, pieces, side, name, tile=512):
    shape = (begun.shape[0] // 2, begun.shape[1])
    return call(
        functools.partial(pass_kernel, side=side, tile=tile),
        name,
        [SM] + [VM] * 5,
        [(shape, F32), (shape, BF)],
        (pick, begun, b, *pieces),
        flops=600_000_000,
        moved=3_000_000,
    )


def own_kernel(pick_ref, a_ref, w_ref, *refs, tile):
    pieces, kept_ref, sent = refs[:8], refs[8], refs[9:]
    size = kept_ref.shape[0]
    half = kept_ref.shape[1] // 2
    for side in range(2):
        b_ref, *weights = pieces[4 * side : 4 * side + 4]
        for j in range(half // tile):
            col = slice(j * tile, (j + 1) * tile)
            at = slice(side * half + j * tile, side * half + (j + 1) * tile)
            total = dot(a_ref[...], w_ref[:, at])
            total = total + across(b_ref, slice(2 * size, 4 * size), *weights, side, col, pick_ref[2])
            kept_ref[:, at] = total[:size]
            first = size
            for out_ref in sent:
                out_ref[:, at] = total[first : first + out_ref.shape[0]].astype(BF)
                first += out_ref.shape[0]


def own_part(pick, a, w, left, right, tile=512):
    size, width = a.shape[0] // 2, w.shape[1]
    sent = (3 * size // 8, 3 * size // 8, size // 4)
    return call(
        functools.partial(own_kernel, tile=tile),
        "own",
        [SM] + [VM] * 10,
        [((size, width), F32)] + [((n, width), BF) for n in sent],
        (pick, a, w, *left, *right),
        flops=2_000_000_000,
        moved=9_000_000,
    )


def join_kernel(a_ref, b_ref, out_ref):
    out_ref[...] = (a_ref[...] + b_ref[...].astype(F32)).astype(BF)


def join(a, b, name):
    return call(join_kernel, name, [VM, VM], [(a.shape, BF)], (a, b), flops=300_000, moved=2_000_000)[0]


def finish_kernel(own_ref, left_ref, right_ref, *refs):
    swaps, out_ref = refs[:-1], refs[-1]
    half = left_ref.shape[1]
    first = 0
    for swap_ref in swaps:
        rows = slice(first, first + swap_ref.shape[0])
        for side, far_ref in enumerate((left_ref, right_ref)):
            at = slice(side * half, (side + 1) * half)
            total = own_ref[rows, at] + swap_ref[:, at].astype(F32) + far_ref[rows, :].astype(F32)
            out_ref[rows, at] = total.astype(BF)
        first = rows.stop


def finish(own, left, right, swaps):
    ins = [VM] * (3 + len(swaps))
    return call(finish_kernel, "finish", ins, [(own.shape, BF)], (own, left, right, *swaps), flops=2_000_000, moved=5_000_000)[0]


def partners(bit, size, inner):
    if 2 << bit == inner:
        flip = inner - 1
    elif 2 << bit == size:
        flip = (size - 1) & ~(inner - 1)
    else:
        flip = 1 << bit
    return [(i, i ^ flip) for i in range(size)]


def body(queries, keys, values, log_decay, level_weight, norm_gain, out_weight):
    rows, heads, _ = queries.shape
    seq_size, head_size = lax.axis_size("seq"), lax.axis_size("head")
    bits = seq_size.bit_length() - 1
    base = (rows // SPAN).bit_length()
    ring = head_size // 2
    pos = lax.axis_index("seq").astype(jnp.int32)
    lane = lax.axis_index("head").astype(jnp.int32)
    x, core = lane // 2, lane % 2
    parity = pos % 2
    near = x ^ 1
    side = (x + ring - 1 + 2 * (x % 2)) % ring
    pick = jnp.stack([pos, core, parity, (x + 2) % ring, near, side, x])
    pos1 = pos[None]
    swap = [(i, i ^ 1) for i in range(head_size)]
    to_near = [(i, i ^ 2) for i in range(head_size)]
    to_side = [(i, (i + (2 if i // 2 % 2 else -2)) % head_size) for i in range(head_size)]
    to_y = [(i, i ^ 1) for i in range(seq_size)]

    flat = lambda a: a.reshape(rows, heads * HD)
    ld = jnp.transpose(log_decay, (1, 0))
    lw = jnp.transpose(level_weight, (2, 1, 0))
    k2, v2 = flat(keys), flat(values)
    pay, cum = summary(ld, k2, v2)

    depth, width = out_weight.shape
    off = jnp.zeros((heads, 128), F32)
    after = cum
    recvs, offs = [], []
    for b in range(bits):
        recv = lax.ppermute(pay, "seq", partners(b, seq_size, 4))
        recvs.append(recv)
        offs.append(off)
        if b == 0:
            weight, _ = lax.optimization_barrier((out_weight, pay))
            mine = lax.dynamic_slice(weight, (depth // 2 + parity * (depth // 4), 0), (depth // 4, width))
            mine_l = lax.ppermute(mine[:, : width // 2], "head", to_near)
            mine_r = lax.ppermute(mine[:, width // 2 :], "head", to_side)
        if b == 1:
            weight, _ = lax.optimization_barrier((out_weight, pay))
            whole_l = lax.ppermute(weight[: depth // 2, : width // 2], "head", to_near)
            whole_r = lax.ppermute(weight[: depth // 2, width // 2 :], "head", to_side)
        if b == 2:
            queries, keys, values, _ = lax.optimization_barrier((queries, keys, values, pay))
            acc, qt = local(flat(queries), flat(keys), flat(values), cum, lw)
            after = acc
        if b == 3:
            mine_l, mine_r, _ = lax.optimization_barrier((mine_l, mine_r, pay))
            theirs = lax.ppermute(jnp.concatenate([mine_l, mine_r], axis=0), "seq", to_y)
        if b >= 3:
            for i in (0, 1, 2) if b == 3 else (3,):
                acc = far(pos1, acc, qt, recvs[i], offs[i], cum, lw, i, base)
            after = acc
        if b < bits - 1:
            pay, off = merge(pos1, after, recv, pay, off, b)
    n_near, n_side, n_own = norm(pick, acc, qt, recv, off, cum, lw, norm_gain, bits - 1, base, ring)
    from_near = lax.ppermute(n_near, "head", to_near)
    from_side = lax.ppermute(n_side, "head", to_side)
    left, right = (whole_l, mine_l, theirs), (whole_r, mine_r, theirs)
    begun_l = start(n_side, out_weight, 0, "start_left")
    begun_r = start(n_near, out_weight, 1, "start_right")
    keep_l, send_l = pass_on(pick, begun_l, from_near, left, 0, "left")
    swap_l = lax.ppermute(send_l, "head", swap)
    keep_r, send_r = pass_on(pick, begun_r, from_side, right, 1, "right")
    swap_r = lax.ppermute(send_r, "head", swap)
    both_l = join(keep_l, swap_l, "join_left")
    both_r = join(keep_r, swap_r, "join_right")
    far_l = lax.ppermute(both_l, "head", to_side)
    far_r = lax.ppermute(both_r, "head", to_near)
    n_own, _, _ = lax.optimization_barrier((n_own, both_l, both_r))
    keep, *sends = own_part(pick, n_own, out_weight, (from_near, *left), (from_side, *right))
    swaps = [lax.ppermute(send, "head", swap) for send in sends]
    return finish(keep, far_l, far_r, swaps)


def solution(mesh):
    return jax.shard_map(
        body,
        mesh=mesh,
        in_specs=(
            P("seq", "head", None),
            P("seq", "head", None),
            P("seq", "head", None),
            P("seq", "head"),
            P("seq", "head", None),
            P("head", None),
            P("head", None),
        ),
        out_specs=P(("seq", "head"), None),
        check_vma=False,
    )
```

```python
import functools
import jax
import jax.numpy as jnp
from jax import lax
from jax.experimental import pallas as pl
from jax.experimental.pallas import tpu as pltpu
from jax.sharding import PartitionSpec as P

SPAN = 64
HD = 128
BF = jnp.bfloat16
F32 = jnp.float32
VMEM_LIMIT = 16 * 1024 * 1024
VM = pl.BlockSpec(memory_space=pltpu.VMEM)
SM = pl.BlockSpec(memory_space=pltpu.SMEM)


def call(kernel, name, ins, outs, args, scratch=(), flops=0, moved=0, **kw):
    return pl.pallas_call(
        kernel,
        in_specs=ins,
        out_specs=[VM] * len(outs),
        out_shape=[jax.ShapeDtypeStruct(shape, dtype) for shape, dtype in outs],
        scratch_shapes=list(scratch),
        compiler_params=pltpu.CompilerParams(vmem_limit_bytes=VMEM_LIMIT),
        cost_estimate=pl.CostEstimate(flops=flops, bytes_accessed=moved, transcendentals=0),
        name=name,
        **kw,
    )(*args)


def dot(a, b):
    return jnp.dot(a, b, preferred_element_type=F32)


def lane_cumsum(x):
    lanes = lax.broadcasted_iota(jnp.int32, (x.shape[0], 128), 1)
    carry = jnp.zeros((x.shape[0], 1), F32)
    chunks = []
    for i in range(x.shape[1] // 128):
        c = x[:, i * 128 : (i + 1) * 128]
        step = 1
        while step < 128:
            c = c + jnp.where(lanes >= step, pltpu.roll(c, step, 1), 0.0)
            step *= 2
        chunks.append(c)
    out = []
    for c in chunks:
        out.append(c + carry)
        carry = carry + c[:, 127:128]
    return jnp.concatenate(out, axis=1)


def total_rows(total):
    high = total.astype(BF).astype(F32)
    mid = (total - high).astype(BF).astype(F32)
    low = total - high - mid
    rows = jnp.concatenate([high, mid, low, jnp.zeros_like(low)], axis=0)
    return rows.astype(BF)


def total_of(ref, heads):
    rows = ref[heads * HD :, :].astype(F32)
    return rows[:heads] + rows[heads : 2 * heads] + rows[2 * heads : 3 * heads]


def summary_kernel(ld_ref, k_ref, v_ref, pay_ref, cum_ref):
    heads = ld_ref.shape[0]
    cum = lane_cumsum(ld_ref[...])
    total = cum[:, -1:]
    cum_ref[...] = cum
    weight = jnp.exp(total - cum)
    pay_ref[heads * HD :, :] = total_rows(jnp.broadcast_to(total, (heads, 128)))
    for h in range(heads):
        at = slice(h * HD, (h + 1) * HD)
        vt = v_ref[:, at].astype(F32).T * weight[h : h + 1]
        pay_ref[at, :] = dot(vt.astype(BF), k_ref[:, at]).astype(BF)


def summary(ld, k, v):
    heads, rows = ld.shape
    return call(
        summary_kernel,
        "summary",
        [VM, VM, VM],
        [((heads * HD + 16, 128), BF), ((heads, rows), F32)],
        (ld, k, v),
        flops=140_000_000,
        moved=2_000_000,
    )


def merge_kernel(pos_ref, after_ref, recv_ref, self_ref, off_ref, pay_out, off_out, *, bit):
    heads = off_ref.shape[0]
    right = ((pos_ref[0] >> bit) & 1).astype(F32)
    there = total_of(recv_ref, heads)
    here = total_of(self_ref, heads)
    off_out[...] = off_ref[...] + right * there
    pay_out[heads * HD :, :] = total_rows(here + there)
    keep = right + (1.0 - right) * jnp.exp(there)
    take = (1.0 - right) + right * jnp.exp(here)
    for h in range(heads):
        block = slice(h * HD, (h + 1) * HD)
        state = self_ref[block, :].astype(F32) * keep[h : h + 1] + recv_ref[block, :].astype(F32) * take[h : h + 1]
        pay_out[block, :] = state.astype(BF)


def merge(pos, after, recv, pay, off, bit):
    return call(
        functools.partial(merge_kernel, bit=bit),
        f"merge{bit}",
        [SM, VM, VM, VM, VM],
        [(pay.shape, BF), (off.shape, F32)],
        (pos, after, recv, pay, off),
        flops=200_000,
        moved=600_000,
    )


def local_kernel(q_ref, k_ref, v_ref, cum_ref, lw_ref, acc_ref, qt_ref):
    heads, rows = cum_ref.shape
    pair = 2 * SPAN
    s_pos = lax.broadcasted_iota(jnp.int32, (pair, pair), 0)
    t_pos = lax.broadcasted_iota(jnp.int32, (pair, pair), 1)
    same = jnp.logical_and(s_pos <= t_pos, (s_pos >= SPAN) == (t_pos >= SPAN))
    cross = jnp.logical_and(s_pos < SPAN, t_pos >= SPAN)
    for h in range(heads):
        head = slice(h * HD, (h + 1) * HD)
        qt_ref[head, :] = q_ref[:, head].astype(F32).T.astype(BF)
        vt = v_ref[:, head].astype(F32).T
        cum = cum_ref[h : h + 1, :]
        weight = lambda level: lw_ref[level, h : h + 1, :]
        for i in range(rows // pair):
            at = slice(i * pair, (i + 1) * pair)
            middle = cum[:, i * pair + SPAN - 1 : i * pair + SPAN]
            grow = jnp.exp(cum[:, at] - middle)
            scores = dot(k_ref[at, head], qt_ref[head, at])
            probs = scores * jnp.where(same, weight(0)[:, at], jnp.where(cross, weight(1)[:, at], 0.0))
            held = (vt[:, at] * jnp.exp(middle - cum[:, at])).astype(BF)
            acc_ref[head, at] = dot(held, probs.astype(BF)) * grow
        level, half = 2, pair
        while half < rows:
            for i in range(rows // (2 * half)):
                left = slice(2 * i * half, (2 * i + 1) * half)
                right = slice((2 * i + 1) * half, (2 * i + 2) * half)
                end = cum[:, left.stop - 1 : left.stop]
                held = (vt[:, left] * jnp.exp(end - cum[:, left])).astype(BF)
                bucket = dot(held, k_ref[left, head]).astype(BF)
                factor = weight(level)[:, right] * jnp.exp(cum[:, right] - end)
                acc_ref[head, right] += dot(bucket, qt_ref[head, right]) * factor
            level, half = level + 1, half * 2


def local(q, k, v, cum, lw):
    heads, rows = cum.shape
    return call(
        local_kernel,
        "local",
        [VM] * 5,
        [((heads * HD, rows), F32), ((heads * HD, rows), BF)],
        (q, k, v, cum, lw),
        flops=1_000_000,
        moved=100_000,
    )


def far_factor(pos_ref, off_ref, cum, weight, head, bit):
    flag = ((pos_ref[0] >> bit) & 1).astype(F32)
    return weight * jnp.exp(off_ref[head : head + 1, :1] + cum) * flag


def far_kernel(pos_ref, acc_ref, qt_ref, recv_ref, off_ref, cum_ref, lw_ref, out_ref, *, bit, base):
    heads, rows = cum_ref.shape
    width = min(256, rows)
    for h in range(heads):
        head = slice(h * HD, (h + 1) * HD)
        for i in range(rows // width):
            at = slice(i * width, (i + 1) * width)
            factor = far_factor(pos_ref, off_ref, cum_ref[h : h + 1, at], lw_ref[base + bit, h : h + 1, at], h, bit)
            out_ref[head, at] = acc_ref[head, at] + dot(recv_ref[head, :], qt_ref[head, at]) * factor


def far(pos, acc, qt, recv, off, cum, lw, bit, base):
    return call(
        functools.partial(far_kernel, bit=bit, base=base),
        f"far{bit}",
        [SM] + [VM] * 6,
        [(acc.shape, F32)],
        (pos, acc, qt, recv, off, cum, lw),
        flops=1_000_000,
        moved=100_000,
        input_output_aliases={1: 0},
    )[0]


def norm_kernel(pick_ref, acc_ref, qt_ref, recv_ref, off_ref, cum_ref, lw_ref, gain_ref, near_ref, side_ref, own_ref, *, bit, base):
    heads = gain_ref.shape[0]
    core = pick_ref[1]
    size = own_ref.shape[0] // 2
    targets = (((near_ref, 0), (side_ref, 0)), ((near_ref, 1),), ((side_ref, 1),), ((own_ref, 0),))
    for i, outs in enumerate(targets):
        start = pick_ref[3 + i] * (2 * size)
        for part, offset in enumerate((core * size, (1 - core) * size)):
            at = pl.ds(pl.multiple_of(start + offset, size), size)
            for h in range(heads):
                head = slice(h * HD, (h + 1) * HD)
                factor = far_factor(pick_ref, off_ref, cum_ref[h : h + 1, at], lw_ref[base + bit, h : h + 1, at], h, bit)
                att = acc_ref[head, at] + dot(recv_ref[head, :], qt_ref[head, at]) * factor
                mean = jnp.mean(att * att, axis=0, keepdims=True)
                normed = ((att * lax.rsqrt(mean + 1e-6)).T * gain_ref[h : h + 1, :]).astype(BF)
                for out_ref, slot in outs:
                    first = (2 * slot + part) * size
                    out_ref[first : first + size, head] = normed


def norm(pick, acc, qt, recv, off, cum, lw, gain, bit, base, ring):
    heads, rows = cum.shape
    size = rows // ring
    return call(
        functools.partial(norm_kernel, bit=bit, base=base),
        "norm",
        [SM] + [VM] * 7,
        [((2 * size, heads * HD), BF)] * 2 + [((size, heads * HD), BF)],
        (pick, acc, qt, recv, off, cum, lw, gain),
        flops=1_000_000,
        moved=100_000,
    )


def begin_kernel(pick_ref, near_ref, side_ref, w_ref, *refs, tile):
    pieces, (out_l, out_r, full_l, full_r) = refs[:6], refs[6:]
    rows, half = out_l.shape
    for side, (a_ref, out_ref, full_ref) in enumerate(((side_ref, out_l, full_l), (near_ref, out_r, full_r))):
        whole_ref, mine_ref, theirs_ref = pieces[3 * side : 3 * side + 3]
        depth, share = whole_ref.shape[0], mine_ref.shape[0]
        first = pick_ref[7 + side]
        full_ref[:depth, :] = whole_ref[...]
        full_ref[pl.ds(pl.multiple_of(depth + first * share, 32), share), :] = mine_ref[...]
        full_ref[pl.ds(pl.multiple_of(depth + (1 - first) * share, 32), share), :] = theirs_ref[...]
        for j in range(half // tile):
            own = slice(side * half + j * tile, side * half + (j + 1) * tile)
            out_ref[:, j * tile : (j + 1) * tile] = dot(a_ref[rows:, :], w_ref[:, own]).astype(BF)


def begin(pick, near, side, w, left, right, tile=512):
    half = w.shape[1] // 2
    return call(
        functools.partial(begin_kernel, tile=tile),
        "begin",
        [SM] + [VM] * 9,
        [((near.shape[0] // 2, half), BF)] * 2 + [((w.shape[0], half), BF)] * 2,
        (pick, near, side, w, *left, *right),
        flops=1_000_000_000,
        moved=6_000_000,
    )


def pass_kernel(begun_ref, b_ref, w_ref, kept_ref, sent_ref, *, tile):
    size, half = kept_ref.shape
    for j in range(half // tile):
        col = slice(j * tile, (j + 1) * tile)
        total = begun_ref[:, col].astype(F32) + dot(b_ref[: 2 * size, :], w_ref[:, col])
        kept_ref[:, col] = total[:size]
        sent_ref[:, col] = total[size:].astype(BF)


def pass_on(begun, b, w, name, tile=512):
    shape = (begun.shape[0] // 2, begun.shape[1])
    return call(
        functools.partial(pass_kernel, tile=tile),
        name,
        [VM] * 3,
        [(shape, F32), (shape, BF)],
        (begun, b, w),
        flops=600_000_000,
        moved=3_000_000,
    )


def own_kernel(a_ref, w_ref, b_left, b_right, w_left, w_right, kept_ref, *sent, tile):
    size = kept_ref.shape[0]
    half = kept_ref.shape[1] // 2
    for side, (b_ref, v_ref) in enumerate(((b_left, w_left), (b_right, w_right))):
        for j in range(half // tile):
            col = slice(j * tile, (j + 1) * tile)
            at = slice(side * half + j * tile, side * half + (j + 1) * tile)
            total = dot(a_ref[...], w_ref[:, at]) + dot(b_ref[2 * size :, :], v_ref[:, col])
            kept_ref[:, at] = total[:size]
            first = size
            for out_ref in sent:
                out_ref[:, at] = total[first : first + out_ref.shape[0]].astype(BF)
                first += out_ref.shape[0]


def own_part(a, w, bs, ws, tile=512):
    size, width = a.shape[0] // 2, w.shape[1]
    sent = (3 * size // 8, 3 * size // 8, size // 4)
    return call(
        functools.partial(own_kernel, tile=tile),
        "own",
        [VM] * 6,
        [((size, width), F32)] + [((n, width), BF) for n in sent],
        (a, w, *bs, *ws),
        flops=2_000_000_000,
        moved=9_000_000,
    )


def join_kernel(a_ref, b_ref, out_ref):
    out_ref[...] = (a_ref[...] + b_ref[...].astype(F32)).astype(BF)


def join(a, b, name):
    return call(join_kernel, name, [VM, VM], [(a.shape, BF)], (a, b), flops=300_000, moved=2_000_000)[0]


def finish_kernel(own_ref, left_ref, right_ref, *refs):
    swaps, out_ref = refs[:-1], refs[-1]
    half = left_ref.shape[1]
    first = 0
    for swap_ref in swaps:
        rows = slice(first, first + swap_ref.shape[0])
        for side, far_ref in enumerate((left_ref, right_ref)):
            at = slice(side * half, (side + 1) * half)
            total = own_ref[rows, at] + swap_ref[:, at].astype(F32) + far_ref[rows, :].astype(F32)
            out_ref[rows, at] = total.astype(BF)
        first = rows.stop


def finish(own, left, right, swaps):
    ins = [VM] * (3 + len(swaps))
    return call(finish_kernel, "finish", ins, [(own.shape, BF)], (own, left, right, *swaps), flops=2_000_000, moved=5_000_000)[0]


def partners(bit, size, inner):
    if 2 << bit == inner:
        flip = inner - 1
    elif 2 << bit == size:
        flip = (size - 1) & ~(inner - 1)
    else:
        flip = 1 << bit
    return [(i, i ^ flip) for i in range(size)]


def body(queries, keys, values, log_decay, level_weight, norm_gain, out_weight):
    rows, heads, _ = queries.shape
    seq_size, head_size = lax.axis_size("seq"), lax.axis_size("head")
    bits = seq_size.bit_length() - 1
    base = (rows // SPAN).bit_length()
    ring = head_size // 2
    pos = lax.axis_index("seq").astype(jnp.int32)
    lane = lax.axis_index("head").astype(jnp.int32)
    x, core = lane // 2, lane % 2
    share_l, share_r = pos % 2, pos // 2 % 2
    near = x ^ 1
    side = (x + ring - 1 + 2 * (x % 2)) % ring
    pick = jnp.stack([pos, core, core, (x + 2) % ring, near, side, x, share_l, share_r])
    pos1 = pos[None]
    swap = [(i, i ^ 1) for i in range(head_size)]
    to_near = [(i, i ^ 2) for i in range(head_size)]
    to_side = [(i, (i + (2 if i // 2 % 2 else -2)) % head_size) for i in range(head_size)]
    to_y = [[(i, i ^ flip) for i in range(seq_size)] for flip in (1, 3)]

    flat = lambda a: a.reshape(rows, heads * HD)
    ld = jnp.transpose(log_decay, (1, 0))
    lw = jnp.transpose(level_weight, (2, 1, 0))
    k2, v2 = flat(keys), flat(values)
    pay, cum = summary(ld, k2, v2)

    depth, width = out_weight.shape
    share = 5 * depth // 16
    direct = depth - 2 * share
    off = jnp.zeros((heads, 128), F32)
    after = cum
    recvs, offs = [], []
    for b in range(bits):
        recv = lax.ppermute(pay, "seq", partners(b, seq_size, 4))
        recvs.append(recv)
        offs.append(off)
        if b == 0:
            weight, _ = lax.optimization_barrier((out_weight, pay))
            mine_l = lax.dynamic_slice(weight, (direct + share_l * share, 0), (share, width // 2))
            mine_r = lax.dynamic_slice(weight, (direct + share_r * share, width // 2), (share, width // 2))
            mine_l = lax.ppermute(mine_l, "head", to_near)
            mine_r = lax.ppermute(mine_r, "head", to_side)
        if b == 1:
            weight, _ = lax.optimization_barrier((out_weight, pay))
            slice_l, slice_r = weight[:direct, : width // 2], weight[:direct, width // 2 :]
            slice_l, slice_r, recv = lax.optimization_barrier((slice_l, slice_r, recv))
            whole_l = lax.ppermute(slice_l, "head", to_near)
        if b == 2:
            queries, keys, values, _ = lax.optimization_barrier((queries, keys, values, pay))
            acc, qt = local(flat(queries), flat(keys), flat(values), cum, lw)
            after = acc
        if b == 3:
            slice_r, _ = lax.optimization_barrier((slice_r, pay))
            whole_r = lax.ppermute(slice_r, "head", to_side)
            mine_l, mine_r, _ = lax.optimization_barrier((mine_l, mine_r, pay))
            theirs_l = lax.ppermute(mine_l, "seq", to_y[0])
            theirs_r = lax.ppermute(mine_r, "seq", to_y[1])
            for i in (0, 1, 2):
                acc = far(pos1, acc, qt, recvs[i], offs[i], cum, lw, i, base)
            after = acc
        if b == 4:
            acc = far(pos1, acc, qt, recvs[3], offs[3], cum, lw, 3, base)
        if b < bits - 1:
            pay, off = merge(pos1, after, recv, pay, off, b)
    n_near, n_side, n_own = norm(pick, acc, qt, recv, off, cum, lw, norm_gain, bits - 1, base, ring)
    from_near = lax.ppermute(n_near, "head", to_near)
    from_side = lax.ppermute(n_side, "head", to_side)
    begun_l, begun_r, w_l, w_r = begin(
        pick, n_near, n_side, out_weight, (whole_l, mine_l, theirs_l), (whole_r, mine_r, theirs_r)
    )
    keep_l, send_l = pass_on(begun_l, from_near, w_l, "left")
    swap_l = lax.ppermute(send_l, "head", swap)
    keep_r, send_r = pass_on(begun_r, from_side, w_r, "right")
    swap_r = lax.ppermute(send_r, "head", swap)
    both_l = join(keep_l, swap_l, "join_left")
    both_r = join(keep_r, swap_r, "join_right")
    far_l = lax.ppermute(both_l, "head", to_side)
    far_r = lax.ppermute(both_r, "head", to_near)
    n_own, _, _ = lax.optimization_barrier((n_own, both_l, both_r))
    keep, *sends = own_part(n_own, out_weight, (from_near, from_side), (w_l, w_r))
    swaps = [lax.ppermute(send, "head", swap) for send in sends]
    return finish(keep, far_l, far_r, swaps)


def solution(mesh):
    return jax.shard_map(
        body,
        mesh=mesh,
        in_specs=(
            P("seq", "head", None),
            P("seq", "head", None),
            P("seq", "head", None),
            P("seq", "head"),
            P("seq", "head", None),
            P("head", None),
            P("head", None),
        ),
        out_specs=P(("seq", "head"), None),
        check_vma=False,
    )
```

```python
import functools
import jax
import jax.numpy as jnp
from jax import lax
from jax.experimental import pallas as pl
from jax.experimental.pallas import tpu as pltpu
from jax.sharding import PartitionSpec as P

SPAN = 64
HD = 128
BF = jnp.bfloat16
F32 = jnp.float32
VM = pl.BlockSpec(memory_space=pltpu.VMEM)
SM = pl.BlockSpec(memory_space=pltpu.SMEM)


def call(kernel, name, ins, outs, args, scratch=(), flops=0, moved=0, vmem=8, **kw):
    return pl.pallas_call(
        kernel,
        in_specs=ins,
        out_specs=[VM] * len(outs),
        out_shape=[jax.ShapeDtypeStruct(shape, dtype) for shape, dtype in outs],
        scratch_shapes=list(scratch),
        compiler_params=pltpu.CompilerParams(vmem_limit_bytes=vmem * 1024 * 1024),
        cost_estimate=pl.CostEstimate(flops=flops, bytes_accessed=moved, transcendentals=0),
        name=name,
        **kw,
    )(*args)


def dot(a, b):
    return jnp.dot(a, b, preferred_element_type=F32)


def lane_cumsum(x):
    lanes = lax.broadcasted_iota(jnp.int32, (x.shape[0], 128), 1)
    carry = jnp.zeros((x.shape[0], 1), F32)
    chunks = []
    for i in range(x.shape[1] // 128):
        c = x[:, i * 128 : (i + 1) * 128]
        step = 1
        while step < 128:
            c = c + jnp.where(lanes >= step, pltpu.roll(c, step, 1), 0.0)
            step *= 2
        chunks.append(c)
    out = []
    for c in chunks:
        out.append(c + carry)
        carry = carry + c[:, 127:128]
    return jnp.concatenate(out, axis=1)


def total_rows(total):
    high = total.astype(BF).astype(F32)
    mid = (total - high).astype(BF).astype(F32)
    low = total - high - mid
    rows = jnp.concatenate([high, mid, low, jnp.zeros_like(low)], axis=0)
    return rows.astype(BF)


def total_of(ref, heads):
    rows = ref[heads * HD :, :].astype(F32)
    return rows[:heads] + rows[heads : 2 * heads] + rows[2 * heads : 3 * heads]


def summary_kernel(ld_ref, k_ref, v_ref, pay_ref, cum_ref):
    heads = ld_ref.shape[0]
    cum = lane_cumsum(ld_ref[...])
    total = cum[:, -1:]
    cum_ref[...] = cum
    weight = jnp.exp(total - cum)
    pay_ref[heads * HD :, :] = total_rows(jnp.broadcast_to(total, (heads, 128)))
    for h in range(heads):
        at = slice(h * HD, (h + 1) * HD)
        vt = v_ref[:, at].astype(F32).T * weight[h : h + 1]
        pay_ref[at, :] = dot(vt.astype(BF), k_ref[:, at]).astype(BF)


def summary(ld, k, v):
    heads, rows = ld.shape
    return call(
        summary_kernel,
        "summary",
        [VM, VM, VM],
        [((heads * HD + 16, 128), BF), ((heads, rows), F32)],
        (ld, k, v),
        flops=140_000_000,
        moved=2_000_000,
    )


def merge_kernel(pos_ref, after_ref, recv_ref, self_ref, off_ref, pay_out, off_out, *, bit):
    heads = off_ref.shape[0]
    right = ((pos_ref[0] >> bit) & 1).astype(F32)
    there = total_of(recv_ref, heads)
    here = total_of(self_ref, heads)
    off_out[...] = off_ref[...] + right * there
    if pay_out.shape[0] > heads * HD:
        pay_out[heads * HD :, :] = total_rows(here + there)
    keep = right + (1.0 - right) * jnp.exp(there)
    take = (1.0 - right) + right * jnp.exp(here)
    for h in range(heads):
        block = slice(h * HD, (h + 1) * HD)
        state = self_ref[block, :].astype(F32) * keep[h : h + 1] + recv_ref[block, :].astype(F32) * take[h : h + 1]
        pay_out[block, :] = state.astype(BF)


def merge(pos, after, recv, pay, off, bit, last):
    return call(
        functools.partial(merge_kernel, bit=bit),
        f"merge{bit}",
        [SM, VM, VM, VM, VM],
        [((off.shape[0] * HD if last else pay.shape[0], HD), BF), (off.shape, F32)],
        (pos, after, recv, pay, off),
        flops=200_000,
        moved=600_000,
        vmem=4,
    )


def local_kernel(q_ref, k_ref, v_ref, cum_ref, lw_ref, acc_ref, qt_ref):
    heads, rows = cum_ref.shape
    pair = 2 * SPAN
    s_pos = lax.broadcasted_iota(jnp.int32, (pair, pair), 0)
    t_pos = lax.broadcasted_iota(jnp.int32, (pair, pair), 1)
    same = jnp.logical_and(s_pos <= t_pos, (s_pos >= SPAN) == (t_pos >= SPAN))
    cross = jnp.logical_and(s_pos < SPAN, t_pos >= SPAN)
    for h in range(heads):
        head = slice(h * HD, (h + 1) * HD)
        qt_ref[head, :] = q_ref[:, head].astype(F32).T.astype(BF)
        vt = v_ref[:, head].astype(F32).T
        cum = cum_ref[h : h + 1, :]
        weight = lambda level: lw_ref[level, h : h + 1, :]
        for i in range(rows // pair):
            at = slice(i * pair, (i + 1) * pair)
            middle = cum[:, i * pair + SPAN - 1 : i * pair + SPAN]
            grow = jnp.exp(cum[:, at] - middle)
            scores = dot(k_ref[at, head], qt_ref[head, at])
            probs = scores * jnp.where(same, weight(0)[:, at], jnp.where(cross, weight(1)[:, at], 0.0))
            held = (vt[:, at] * jnp.exp(middle - cum[:, at])).astype(BF)
            acc_ref[head, at] = dot(held, probs.astype(BF)) * grow
        level, half = 2, pair
        while half < rows:
            for i in range(rows // (2 * half)):
                left = slice(2 * i * half, (2 * i + 1) * half)
                right = slice((2 * i + 1) * half, (2 * i + 2) * half)
                end = cum[:, left.stop - 1 : left.stop]
                held = (vt[:, left] * jnp.exp(end - cum[:, left])).astype(BF)
                bucket = dot(held, k_ref[left, head]).astype(BF)
                factor = weight(level)[:, right] * jnp.exp(cum[:, right] - end)
                acc_ref[head, right] += dot(bucket, qt_ref[head, right]) * factor
            level, half = level + 1, half * 2


def local(q, k, v, cum, lw):
    heads, rows = cum.shape
    return call(
        local_kernel,
        "local",
        [VM] * 5,
        [((heads * HD, rows), F32), ((heads * HD, rows), BF)],
        (q, k, v, cum, lw),
        flops=1_000_000,
        moved=100_000,
        vmem=12,
    )


def far_factor(pos_ref, off_ref, cum, weight, head, bit):
    flag = ((pos_ref[0] >> bit) & 1).astype(F32)
    return weight * jnp.exp(off_ref[head : head + 1, :1] + cum) * flag


def far_kernel(pos_ref, acc_ref, qt_ref, recv_ref, off_ref, cum_ref, lw_ref, out_ref, *, bit, base):
    heads, rows = cum_ref.shape
    width = min(256, rows)
    for h in range(heads):
        head = slice(h * HD, (h + 1) * HD)
        for i in range(rows // width):
            at = slice(i * width, (i + 1) * width)
            factor = far_factor(pos_ref, off_ref, cum_ref[h : h + 1, at], lw_ref[base + bit, h : h + 1, at], h, bit)
            out_ref[head, at] = acc_ref[head, at] + dot(recv_ref[head, :], qt_ref[head, at]) * factor


def far(pos, acc, qt, recv, off, cum, lw, bit, base):
    return call(
        functools.partial(far_kernel, bit=bit, base=base),
        f"far{bit}",
        [SM] + [VM] * 6,
        [(acc.shape, F32)],
        (pos, acc, qt, recv, off, cum, lw),
        flops=1_000_000,
        moved=100_000,
        input_output_aliases={1: 0},
    )[0]


def norm_kernel(pick_ref, acc_ref, qt_ref, recv_ref, off_ref, cum_ref, lw_ref, gain_ref, near_ref, side_ref, own_ref, *, bit, base):
    heads = gain_ref.shape[0]
    core = pick_ref[1]
    size = own_ref.shape[0] // 2
    targets = (((near_ref, 0), (side_ref, 0)), ((near_ref, 1),), ((side_ref, 1),), ((own_ref, 0),))
    for i, outs in enumerate(targets):
        start = pick_ref[3 + i] * (2 * size)
        for part, offset in enumerate((core * size, (1 - core) * size)):
            at = pl.ds(pl.multiple_of(start + offset, size), size)
            for h in range(heads):
                head = slice(h * HD, (h + 1) * HD)
                factor = far_factor(pick_ref, off_ref, cum_ref[h : h + 1, at], lw_ref[base + bit, h : h + 1, at], h, bit)
                att = acc_ref[head, at] + dot(recv_ref[head, :], qt_ref[head, at]) * factor
                mean = jnp.mean(att * att, axis=0, keepdims=True)
                normed = ((att * lax.rsqrt(mean + 1e-6)).T * gain_ref[h : h + 1, :]).astype(BF)
                for out_ref, slot in outs:
                    first = (2 * slot + part) * size
                    out_ref[first : first + size, head] = normed


def norm(pick, acc, qt, recv, off, cum, lw, gain, bit, base, ring):
    heads, rows = cum.shape
    size = rows // ring
    return call(
        functools.partial(norm_kernel, bit=bit, base=base),
        "norm",
        [SM] + [VM] * 7,
        [((2 * size, heads * HD), BF)] * 2 + [((size, heads * HD), BF)],
        (pick, acc, qt, recv, off, cum, lw, gain),
        flops=1_000_000,
        moved=100_000,
        vmem=10,
    )


def begin_kernel(pick_ref, near_ref, side_ref, w_ref, *refs, tile):
    pieces, (out_l, out_r, full_l, full_r) = refs[:6], refs[6:]
    rows, half = out_l.shape
    for side, (a_ref, out_ref, full_ref) in enumerate(((side_ref, out_l, full_l), (near_ref, out_r, full_r))):
        whole_ref, mine_ref, theirs_ref = pieces[3 * side : 3 * side + 3]
        depth, share = whole_ref.shape[0], mine_ref.shape[0]
        first = pick_ref[7 + side]
        full_ref[:depth, :] = whole_ref[...]
        full_ref[pl.ds(pl.multiple_of(depth + first * share, 32), share), :] = mine_ref[...]
        full_ref[pl.ds(pl.multiple_of(depth + (1 - first) * share, 32), share), :] = theirs_ref[...]
        for j in range(half // tile):
            own = slice(side * half + j * tile, side * half + (j + 1) * tile)
            out_ref[:, j * tile : (j + 1) * tile] = dot(a_ref[rows:, :], w_ref[:, own]).astype(BF)


def begin(pick, near, side, w, left, right, tile=512):
    half = w.shape[1] // 2
    return call(
        functools.partial(begin_kernel, tile=tile),
        "begin",
        [SM] + [VM] * 9,
        [((near.shape[0] // 2, half), BF)] * 2 + [((w.shape[0], half), BF)] * 2,
        (pick, near, side, w, *left, *right),
        flops=1_000_000_000,
        moved=6_000_000,
        vmem=20,
    )


def pass_kernel(begun_ref, b_ref, w_ref, kept_ref, sent_ref, *, tile):
    size, half = kept_ref.shape
    for j in range(half // tile):
        col = slice(j * tile, (j + 1) * tile)
        total = begun_ref[:, col].astype(F32) + dot(b_ref[: 2 * size, :], w_ref[:, col])
        kept_ref[:, col] = total[:size]
        sent_ref[:, col] = total[size:].astype(BF)


def pass_on(begun, b, w, name, tile=512):
    shape = (begun.shape[0] // 2, begun.shape[1])
    return call(
        functools.partial(pass_kernel, tile=tile),
        name,
        [VM] * 3,
        [(shape, F32), (shape, BF)],
        (begun, b, w),
        flops=600_000_000,
        moved=3_000_000,
    )


def own_kernel(a_ref, w_ref, b_left, b_right, w_left, w_right, kept_ref, *sent, tile):
    size = kept_ref.shape[0]
    half = kept_ref.shape[1] // 2
    for side, (b_ref, v_ref) in enumerate(((b_left, w_left), (b_right, w_right))):
        for j in range(half // tile):
            col = slice(j * tile, (j + 1) * tile)
            at = slice(side * half + j * tile, side * half + (j + 1) * tile)
            total = dot(a_ref[...], w_ref[:, at]) + dot(b_ref[2 * size :, :], v_ref[:, col])
            kept_ref[:, at] = total[:size]
            first = size
            for out_ref in sent:
                out_ref[:, at] = total[first : first + out_ref.shape[0]].astype(BF)
                first += out_ref.shape[0]


def own_part(a, w, bs, ws, tile=512):
    size, width = a.shape[0] // 2, w.shape[1]
    sent = (3 * size // 8, 3 * size // 8, size // 4)
    return call(
        functools.partial(own_kernel, tile=tile),
        "own",
        [VM] * 6,
        [((size, width), F32)] + [((n, width), BF) for n in sent],
        (a, w, *bs, *ws),
        flops=2_000_000_000,
        moved=9_000_000,
        vmem=16,
    )


def join_kernel(a_ref, b_ref, out_ref):
    out_ref[...] = (a_ref[...] + b_ref[...].astype(F32)).astype(BF)


def join(a, b, name):
    return call(join_kernel, name, [VM, VM], [(a.shape, BF)], (a, b), flops=300_000, moved=2_000_000)[0]


def finish_kernel(own_ref, left_ref, right_ref, *refs, parts):
    swaps, (out_ref, tile_ref, sems) = refs[:3], refs[3:]
    half = left_ref.shape[1]
    size = tile_ref.shape[0] // parts
    copies = []
    first = 0
    for swap_ref in swaps:
        for row in range(0, swap_ref.shape[0], size):
            here = slice(first, first + size)
            for side, far_ref in enumerate((left_ref, right_ref)):
                at = slice(side * half, (side + 1) * half)
                total = own_ref[here, at] + swap_ref[row : row + size, at].astype(F32)
                tile_ref[here, at] = (total + far_ref[here, :].astype(F32)).astype(BF)
            copy = pltpu.make_async_copy(tile_ref.at[here], out_ref.at[here], sems.at[len(copies)])
            copy.start()
            copies.append(copy)
            first += size
    for copy in copies:
        copy.wait()


def finish(own, left, right, swaps, parts=8):
    return pl.pallas_call(
        functools.partial(finish_kernel, parts=parts),
        in_specs=[VM] * 6,
        out_specs=pl.BlockSpec(memory_space=pl.ANY),
        out_shape=jax.ShapeDtypeStruct(own.shape, BF),
        scratch_shapes=[pltpu.VMEM(own.shape, BF), pltpu.SemaphoreType.DMA((parts,))],
        compiler_params=pltpu.CompilerParams(vmem_limit_bytes=8 * 1024 * 1024),
        name="finish",
        cost_estimate=pl.CostEstimate(flops=2_000_000, bytes_accessed=5_000_000, transcendentals=0),
    )(own, left, right, *swaps)


def partners(bit, size, inner):
    if 2 << bit == inner:
        flip = inner - 1
    elif 2 << bit == size:
        flip = 3 * size // 4
    else:
        flip = 1 << bit
    return [(i, i ^ flip) for i in range(size)]


def body(queries, keys, values, log_decay, level_weight, norm_gain, out_weight):
    rows, heads, _ = queries.shape
    seq_size, head_size = lax.axis_size("seq"), lax.axis_size("head")
    bits = seq_size.bit_length() - 1
    base = (rows // SPAN).bit_length()
    ring = head_size // 2
    pos = lax.axis_index("seq").astype(jnp.int32)
    lane = lax.axis_index("head").astype(jnp.int32)
    x, core = lane // 2, lane % 2
    share_l, share_r = pos % 2, pos // 2 % 2
    near = x ^ 1
    side = (x + ring - 1 + 2 * (x % 2)) % ring
    pick = jnp.stack([pos, core, core, (x + 2) % ring, near, side, x, share_l, share_r])
    pos1 = pos[None]
    swap = [(i, i ^ 1) for i in range(head_size)]
    to_near = [(i, i ^ 2) for i in range(head_size)]
    to_side = [(i, (i + (2 if i // 2 % 2 else -2)) % head_size) for i in range(head_size)]
    to_y = [[(i, i ^ flip) for i in range(seq_size)] for flip in (1, 3)]

    flat = lambda a: a.reshape(rows, heads * HD)
    ld = jnp.transpose(log_decay, (1, 0))
    lw = jnp.transpose(level_weight, (2, 1, 0))
    k2, v2 = flat(keys), flat(values)
    pay, cum = summary(ld, k2, v2)

    depth, width = out_weight.shape
    share = 5 * depth // 16
    direct = depth - 2 * share
    off = jnp.zeros((heads, 128), F32)
    after = cum
    recvs, offs = [], []
    for b in range(bits):
        recv = lax.ppermute(pay, "seq", partners(b, seq_size, 4))
        recvs.append(recv)
        offs.append(off)
        if b == 0:
            weight, _ = lax.optimization_barrier((out_weight, pay))
            mine_l = lax.dynamic_slice(weight, (direct + share_l * share, 0), (share, width // 2))
            mine_r = lax.dynamic_slice(weight, (direct + share_r * share, width // 2), (share, width // 2))
            mine_l = lax.ppermute(mine_l, "head", to_near)
            mine_r = lax.ppermute(mine_r, "head", to_side)
        if b == 1:
            weight, _ = lax.optimization_barrier((out_weight, pay))
            slice_l, slice_r = weight[:direct, : width // 2], weight[:direct, width // 2 :]
            slice_l, slice_r, recv = lax.optimization_barrier((slice_l, slice_r, recv))
            whole_l = lax.ppermute(slice_l, "head", to_near)
        if b == 2:
            queries, keys, values, _ = lax.optimization_barrier((queries, keys, values, pay))
            acc, qt = local(flat(queries), flat(keys), flat(values), cum, lw)
            after = acc
        if b == 3:
            slice_r, _ = lax.optimization_barrier((slice_r, pay))
            whole_r = lax.ppermute(slice_r, "head", to_side)
            mine_l, mine_r, _ = lax.optimization_barrier((mine_l, mine_r, pay))
            theirs_l = lax.ppermute(mine_l, "seq", to_y[0])
            theirs_r = lax.ppermute(mine_r, "seq", to_y[1])
            for i in (0, 1, 2):
                acc = far(pos1, acc, qt, recvs[i], offs[i], cum, lw, i, base)
            after = acc
        if b == 4:
            acc = far(pos1, acc, qt, recvs[3], offs[3], cum, lw, 3, base)
        if b < bits - 1:
            pay, off = merge(pos1, after, recv, pay, off, b, b == bits - 2)
    n_near, n_side, n_own = norm(pick, acc, qt, recv, off, cum, lw, norm_gain, bits - 1, base, ring)
    from_near = lax.ppermute(n_near, "head", to_near)
    from_side = lax.ppermute(n_side, "head", to_side)
    begun_l, begun_r, w_l, w_r = begin(
        pick, n_near, n_side, out_weight, (whole_l, mine_l, theirs_l), (whole_r, mine_r, theirs_r)
    )
    keep_l, send_l = pass_on(begun_l, from_near, w_l, "left")
    swap_l = lax.ppermute(send_l, "head", swap)
    keep_r, send_r = pass_on(begun_r, from_side, w_r, "right")
    swap_r = lax.ppermute(send_r, "head", swap)
    both_l = join(keep_l, swap_l, "join_left")
    both_r = join(keep_r, swap_r, "join_right")
    far_l = lax.ppermute(both_l, "head", to_side)
    far_r = lax.ppermute(both_r, "head", to_near)
    n_own, _, _ = lax.optimization_barrier((n_own, both_l, both_r))
    keep, *sends = own_part(n_own, out_weight, (from_near, from_side), (w_l, w_r))
    swaps = [lax.ppermute(send, "head", swap) for send in sends]
    return finish(keep, far_l, far_r, swaps)


def solution(mesh):
    return jax.shard_map(
        body,
        mesh=mesh,
        in_specs=(
            P("seq", "head", None),
            P("seq", "head", None),
            P("seq", "head", None),
            P("seq", "head"),
            P("seq", "head", None),
            P("head", None),
            P("head", None),
        ),
        out_specs=P(("seq", "head"), None),
        check_vma=False,
    )
```

```python
import functools
import jax
import jax.numpy as jnp
from jax import lax
from jax.experimental import pallas as pl
from jax.experimental.pallas import tpu as pltpu
from jax.sharding import PartitionSpec as P

SPAN = 64
HD = 128
BF = jnp.bfloat16
F32 = jnp.float32
VM = pl.BlockSpec(memory_space=pltpu.VMEM)
SM = pl.BlockSpec(memory_space=pltpu.SMEM)


def call(kernel, name, ins, outs, args, scratch=(), flops=0, moved=0, vmem=8, **kw):
    return pl.pallas_call(
        kernel,
        in_specs=ins,
        out_specs=[VM] * len(outs),
        out_shape=[jax.ShapeDtypeStruct(shape, dtype) for shape, dtype in outs],
        scratch_shapes=list(scratch),
        compiler_params=pltpu.CompilerParams(vmem_limit_bytes=vmem * 1024 * 1024),
        cost_estimate=pl.CostEstimate(flops=flops, bytes_accessed=moved, transcendentals=0),
        name=name,
        **kw,
    )(*args)


def dot(a, b):
    return jnp.dot(a, b, preferred_element_type=F32)


def lane_cumsum(x):
    lanes = lax.broadcasted_iota(jnp.int32, (x.shape[0], 128), 1)
    carry = jnp.zeros((x.shape[0], 1), F32)
    chunks = []
    for i in range(x.shape[1] // 128):
        c = x[:, i * 128 : (i + 1) * 128]
        step = 1
        while step < 128:
            c = c + jnp.where(lanes >= step, pltpu.roll(c, step, 1), 0.0)
            step *= 2
        chunks.append(c)
    out = []
    for c in chunks:
        out.append(c + carry)
        carry = carry + c[:, 127:128]
    return jnp.concatenate(out, axis=1)


def total_rows(total):
    high = total.astype(BF).astype(F32)
    mid = (total - high).astype(BF).astype(F32)
    low = total - high - mid
    rows = jnp.concatenate([high, mid, low, jnp.zeros_like(low)], axis=0)
    return rows.astype(BF)


def total_of(ref, heads):
    rows = ref[heads * HD :, :].astype(F32)
    return rows[:heads] + rows[heads : 2 * heads] + rows[2 * heads : 3 * heads]


def summary_kernel(ld_ref, k_ref, v_ref, pay_ref, cum_ref):
    heads = ld_ref.shape[0]
    cum = lane_cumsum(ld_ref[...])
    total = cum[:, -1:]
    cum_ref[...] = cum
    weight = jnp.exp(total - cum)
    pay_ref[heads * HD :, :] = total_rows(jnp.broadcast_to(total, (heads, 128)))
    for h in range(heads):
        at = slice(h * HD, (h + 1) * HD)
        vt = v_ref[:, at].astype(F32).T * weight[h : h + 1]
        pay_ref[at, :] = dot(vt.astype(BF), k_ref[:, at]).astype(BF)


def summary(ld, k, v):
    heads, rows = ld.shape
    return call(
        summary_kernel,
        "summary",
        [VM, VM, VM],
        [((heads * HD + 16, 128), BF), ((heads, rows), F32)],
        (ld, k, v),
        flops=140_000_000,
        moved=2_000_000,
    )


def merge_kernel(pos_ref, after_ref, recv_ref, self_ref, off_ref, pay_out, off_out, *, bit):
    heads = off_ref.shape[0]
    right = ((pos_ref[0] >> bit) & 1).astype(F32)
    there = total_of(recv_ref, heads)
    here = total_of(self_ref, heads)
    off_out[...] = off_ref[...] + right * there
    if pay_out.shape[0] > heads * HD:
        pay_out[heads * HD :, :] = total_rows(here + there)
    keep = right + (1.0 - right) * jnp.exp(there)
    take = (1.0 - right) + right * jnp.exp(here)
    for h in range(heads):
        block = slice(h * HD, (h + 1) * HD)
        state = self_ref[block, :].astype(F32) * keep[h : h + 1] + recv_ref[block, :].astype(F32) * take[h : h + 1]
        pay_out[block, :] = state.astype(BF)


def merge(pos, after, recv, pay, off, bit, last):
    return call(
        functools.partial(merge_kernel, bit=bit),
        f"merge{bit}",
        [SM, VM, VM, VM, VM],
        [((off.shape[0] * HD if last else pay.shape[0], HD), BF), (off.shape, F32)],
        (pos, after, recv, pay, off),
        flops=200_000,
        moved=600_000,
        vmem=4,
    )


def local_kernel(q_ref, k_ref, v_ref, cum_ref, lw_ref, acc_ref, qt_ref):
    heads, rows = cum_ref.shape
    pair = 2 * SPAN
    s_pos = lax.broadcasted_iota(jnp.int32, (pair, pair), 0)
    t_pos = lax.broadcasted_iota(jnp.int32, (pair, pair), 1)
    same = jnp.logical_and(s_pos <= t_pos, (s_pos >= SPAN) == (t_pos >= SPAN))
    cross = jnp.logical_and(s_pos < SPAN, t_pos >= SPAN)
    for h in range(heads):
        head = slice(h * HD, (h + 1) * HD)
        qt_ref[head, :] = q_ref[:, head].astype(F32).T.astype(BF)
        vt = v_ref[:, head].astype(F32).T
        cum = cum_ref[h : h + 1, :]
        weight = lambda level: lw_ref[level, h : h + 1, :]
        for i in range(rows // pair):
            at = slice(i * pair, (i + 1) * pair)
            middle = cum[:, i * pair + SPAN - 1 : i * pair + SPAN]
            grow = jnp.exp(cum[:, at] - middle)
            scores = dot(k_ref[at, head], qt_ref[head, at])
            probs = scores * jnp.where(same, weight(0)[:, at], jnp.where(cross, weight(1)[:, at], 0.0))
            held = (vt[:, at] * jnp.exp(middle - cum[:, at])).astype(BF)
            acc_ref[head, at] = dot(held, probs.astype(BF)) * grow
        level, half = 2, pair
        while half < rows:
            for i in range(rows // (2 * half)):
                left = slice(2 * i * half, (2 * i + 1) * half)
                right = slice((2 * i + 1) * half, (2 * i + 2) * half)
                end = cum[:, left.stop - 1 : left.stop]
                held = (vt[:, left] * jnp.exp(end - cum[:, left])).astype(BF)
                bucket = dot(held, k_ref[left, head]).astype(BF)
                factor = weight(level)[:, right] * jnp.exp(cum[:, right] - end)
                acc_ref[head, right] += dot(bucket, qt_ref[head, right]) * factor
            level, half = level + 1, half * 2


def local(q, k, v, cum, lw):
    heads, rows = cum.shape
    return call(
        local_kernel,
        "local",
        [VM] * 5,
        [((heads * HD, rows), F32), ((heads * HD, rows), BF)],
        (q, k, v, cum, lw),
        flops=1_000_000,
        moved=100_000,
        vmem=12,
    )


def far_factor(pos_ref, off_ref, cum, weight, head, bit):
    flag = ((pos_ref[0] >> bit) & 1).astype(F32)
    return weight * jnp.exp(off_ref[head : head + 1, :1] + cum) * flag


def far_kernel(pos_ref, acc_ref, qt_ref, recv_ref, off_ref, cum_ref, lw_ref, out_ref, *, bit, base):
    heads, rows = cum_ref.shape
    width = min(256, rows)
    for h in range(heads):
        head = slice(h * HD, (h + 1) * HD)
        for i in range(rows // width):
            at = slice(i * width, (i + 1) * width)
            factor = far_factor(pos_ref, off_ref, cum_ref[h : h + 1, at], lw_ref[base + bit, h : h + 1, at], h, bit)
            out_ref[head, at] = acc_ref[head, at] + dot(recv_ref[head, :], qt_ref[head, at]) * factor


def far(pos, acc, qt, recv, off, cum, lw, bit, base):
    return call(
        functools.partial(far_kernel, bit=bit, base=base),
        f"far{bit}",
        [SM] + [VM] * 6,
        [(acc.shape, F32)],
        (pos, acc, qt, recv, off, cum, lw),
        flops=1_000_000,
        moved=100_000,
        input_output_aliases={1: 0},
    )[0]


def norm_kernel(pick_ref, acc_ref, qt_ref, recv_ref, off_ref, cum_ref, lw_ref, gain_ref, near_ref, side_ref, own_ref, *, bit, base):
    heads = gain_ref.shape[0]
    core = pick_ref[1]
    size = own_ref.shape[0] // 2
    targets = (((near_ref, 0), (side_ref, 0)), ((near_ref, 1),), ((side_ref, 1),), ((own_ref, 0),))
    for i, outs in enumerate(targets):
        start = pick_ref[3 + i] * (2 * size)
        for part, offset in enumerate((core * size, (1 - core) * size)):
            at = pl.ds(pl.multiple_of(start + offset, size), size)
            for h in range(heads):
                head = slice(h * HD, (h + 1) * HD)
                factor = far_factor(pick_ref, off_ref, cum_ref[h : h + 1, at], lw_ref[base + bit, h : h + 1, at], h, bit)
                att = acc_ref[head, at] + dot(recv_ref[head, :], qt_ref[head, at]) * factor
                mean = jnp.mean(att * att, axis=0, keepdims=True)
                normed = ((att * lax.rsqrt(mean + 1e-6)).T * gain_ref[h : h + 1, :]).astype(BF)
                for out_ref, slot in outs:
                    first = (2 * slot + part) * size
                    out_ref[first : first + size, head] = normed


def norm(pick, acc, qt, recv, off, cum, lw, gain, bit, base, ring):
    heads, rows = cum.shape
    size = rows // ring
    return call(
        functools.partial(norm_kernel, bit=bit, base=base),
        "norm",
        [SM] + [VM] * 7,
        [((2 * size, heads * HD), BF)] * 2 + [((size, heads * HD), BF)],
        (pick, acc, qt, recv, off, cum, lw, gain),
        flops=1000000000,
        moved=100_000,
        vmem=10,
    )


def begin_kernel(near_ref, side_ref, w_ref, out_l, out_r, *, tile):
    rows, half = out_l.shape
    for side, (a_ref, out_ref) in enumerate(((side_ref, out_l), (near_ref, out_r))):
        for j in range(half // tile):
            own = slice(side * half + j * tile, side * half + (j + 1) * tile)
            out_ref[:, j * tile : (j + 1) * tile] = dot(a_ref[rows:, :], w_ref[:, own]).astype(BF)


def begin(near, side, w, tile=512):
    return call(
        functools.partial(begin_kernel, tile=tile),
        "begin",
        [VM] * 3,
        [((near.shape[0] // 2, w.shape[1] // 2), BF)] * 2,
        (near, side, w),
        flops=1_000_000,
        moved=100_000,
        vmem=16,
    )


def gather_kernel(pick_ref, *refs):
    for side, full_ref in enumerate(refs[6:]):
        whole_ref, mine_ref, theirs_ref = refs[3 * side : 3 * side + 3]
        depth, share = whole_ref.shape[0], mine_ref.shape[0]
        first = pick_ref[7 + side]
        full_ref[:depth, :] = whole_ref[...]
        full_ref[pl.ds(pl.multiple_of(depth + first * share, 16), share), :] = mine_ref[...]
        full_ref[pl.ds(pl.multiple_of(depth + (1 - first) * share, 16), share), :] = theirs_ref[...]


def gather(pick, left, right):
    depth = left[0].shape[0] + 2 * left[1].shape[0]
    return call(
        gather_kernel,
        "gather",
        [SM] + [VM] * 6,
        [((depth, left[0].shape[1]), BF)] * 2,
        (pick, *left, *right),
        flops=1_000_000,
        moved=100_000,
        vmem=16,
    )


def pass_kernel(begun_ref, b_ref, w_ref, kept_ref, sent_ref, *, tile):
    size, half = kept_ref.shape
    for j in range(half // tile):
        col = slice(j * tile, (j + 1) * tile)
        total = begun_ref[:, col].astype(F32) + dot(b_ref[: 2 * size, :], w_ref[:, col])
        kept_ref[:, col] = total[:size]
        sent_ref[:, col] = total[size:].astype(BF)


def pass_on(begun, b, w, name, tile=512):
    shape = (begun.shape[0] // 2, begun.shape[1])
    return call(
        functools.partial(pass_kernel, tile=tile),
        name,
        [VM] * 3,
        [(shape, F32), (shape, BF)],
        (begun, b, w),
        flops=600_000_000,
        moved=3_000_000,
    )


def own_kernel(a_ref, w_ref, b_left, b_right, w_left, w_right, kept_ref, *sent, tile):
    size = kept_ref.shape[0]
    half = kept_ref.shape[1] // 2
    for side, (b_ref, v_ref) in enumerate(((b_left, w_left), (b_right, w_right))):
        for j in range(half // tile):
            col = slice(j * tile, (j + 1) * tile)
            at = slice(side * half + j * tile, side * half + (j + 1) * tile)
            total = dot(a_ref[...], w_ref[:, at]) + dot(b_ref[2 * size :, :], v_ref[:, col])
            kept_ref[:, at] = total[:size]
            first = size
            for out_ref in sent:
                out_ref[:, at] = total[first : first + out_ref.shape[0]].astype(BF)
                first += out_ref.shape[0]


def own_part(a, w, bs, ws, tile=512):
    size, width = a.shape[0] // 2, w.shape[1]
    sent = (3 * size // 8, 3 * size // 8, size // 4)
    return call(
        functools.partial(own_kernel, tile=tile),
        "own",
        [VM] * 6,
        [((size, width), F32)] + [((n, width), BF) for n in sent],
        (a, w, *bs, *ws),
        flops=2_000_000_000,
        moved=9_000_000,
        vmem=16,
    )


def join_kernel(a_ref, b_ref, out_ref):
    out_ref[...] = (a_ref[...] + b_ref[...].astype(F32)).astype(BF)


def join(a, b, name):
    return call(join_kernel, name, [VM, VM], [(a.shape, BF)], (a, b), flops=300_000, moved=2_000_000)[0]


def finish_kernel(own_ref, left_ref, right_ref, *refs, parts):
    swaps, (out_ref, tile_ref, sems) = refs[:3], refs[3:]
    half = left_ref.shape[1]
    size = tile_ref.shape[0] // parts
    copies = []
    first = 0
    for swap_ref in swaps:
        for row in range(0, swap_ref.shape[0], size):
            here = slice(first, first + size)
            for side, far_ref in enumerate((left_ref, right_ref)):
                at = slice(side * half, (side + 1) * half)
                total = own_ref[here, at] + swap_ref[row : row + size, at].astype(F32)
                tile_ref[here, at] = (total + far_ref[here, :].astype(F32)).astype(BF)
            copy = pltpu.make_async_copy(tile_ref.at[here], out_ref.at[here], sems.at[len(copies)])
            copy.start()
            copies.append(copy)
            first += size
    for copy in copies:
        copy.wait()


def finish(own, left, right, swaps, parts=8):
    return pl.pallas_call(
        functools.partial(finish_kernel, parts=parts),
        in_specs=[VM] * 6,
        out_specs=pl.BlockSpec(memory_space=pl.ANY),
        out_shape=jax.ShapeDtypeStruct(own.shape, BF),
        scratch_shapes=[pltpu.VMEM(own.shape, BF), pltpu.SemaphoreType.DMA((parts,))],
        compiler_params=pltpu.CompilerParams(vmem_limit_bytes=8 * 1024 * 1024),
        name="finish",
        cost_estimate=pl.CostEstimate(flops=2_000_000, bytes_accessed=5_000_000, transcendentals=0),
    )(own, left, right, *swaps)


def partners(bit, size, inner):
    if 2 << bit == inner:
        flip = inner - 1
    elif 2 << bit == size:
        flip = 3 * size // 4
    else:
        flip = 1 << bit
    return [(i, i ^ flip) for i in range(size)]


def body(queries, keys, values, log_decay, level_weight, norm_gain, out_weight):
    rows, heads, _ = queries.shape
    seq_size, head_size = lax.axis_size("seq"), lax.axis_size("head")
    bits = seq_size.bit_length() - 1
    base = (rows // SPAN).bit_length()
    ring = head_size // 2
    pos = lax.axis_index("seq").astype(jnp.int32)
    lane = lax.axis_index("head").astype(jnp.int32)
    x, core = lane // 2, lane % 2
    share_l, share_r = pos % 2, pos // 2 % 2
    near = x ^ 1
    side = (x + ring - 1 + 2 * (x % 2)) % ring
    pick = jnp.stack([pos, core, core, (x + 2) % ring, near, side, x, share_l, share_r])
    pos1 = pos[None]
    swap = [(i, i ^ 1) for i in range(head_size)]
    to_near = [(i, i ^ 2) for i in range(head_size)]
    to_side = [(i, (i + (2 if i // 2 % 2 else -2)) % head_size) for i in range(head_size)]
    to_y = [[(i, i ^ flip) for i in range(seq_size)] for flip in (1, 3)]

    flat = lambda a: a.reshape(rows, heads * HD)
    ld = jnp.transpose(log_decay, (1, 0))
    lw = jnp.transpose(level_weight, (2, 1, 0))
    k2, v2 = flat(keys), flat(values)
    pay, cum = summary(ld, k2, v2)

    depth, width = out_weight.shape
    share = 5 * depth // 16
    direct = depth - 2 * share
    off = jnp.zeros((heads, 128), F32)
    after = cum
    recvs, offs = [], []
    for b in range(bits):
        recv = lax.ppermute(pay, "seq", partners(b, seq_size, 4))
        recvs.append(recv)
        offs.append(off)
        if b == 0:
            weight, _ = lax.optimization_barrier((out_weight, pay))
            mine_l = lax.dynamic_slice(weight, (direct + share_l * share, 0), (share, width // 2))
            mine_r = lax.dynamic_slice(weight, (direct + share_r * share, width // 2), (share, width // 2))
            mine_l = lax.ppermute(mine_l, "head", to_near)
            mine_r = lax.ppermute(mine_r, "head", to_side)
        if b == 1:
            weight, _ = lax.optimization_barrier((out_weight, pay))
            slice_l, slice_r = weight[:direct, : width // 2], weight[:direct, width // 2 :]
            slice_l, slice_r, recv = lax.optimization_barrier((slice_l, slice_r, recv))
            whole_l = lax.ppermute(slice_l, "head", to_near)
        if b == 2:
            queries, keys, values, _ = lax.optimization_barrier((queries, keys, values, pay))
            acc, qt = local(flat(queries), flat(keys), flat(values), cum, lw)
            after = acc
        if b == 3:
            slice_r, _ = lax.optimization_barrier((slice_r, pay))
            whole_r = lax.ppermute(slice_r, "head", to_side)
            for i in (0, 1, 2):
                acc = far(pos1, acc, qt, recvs[i], offs[i], cum, lw, i, base)
            after = acc
        if b == 4:
            mine_l, mine_r, _ = lax.optimization_barrier((mine_l, mine_r, pay))
            theirs_l = lax.ppermute(mine_l, "seq", to_y[0])
            theirs_r = lax.ppermute(mine_r, "seq", to_y[1])
            acc = far(pos1, acc, qt, recvs[3], offs[3], cum, lw, 3, base)
        if b < bits - 1:
            pay, off = merge(pos1, after, recv, pay, off, b, b == bits - 2)
    n_near, n_side, n_own = norm(pick, acc, qt, recv, off, cum, lw, norm_gain, bits - 1, base, ring)
    from_near = lax.ppermute(n_near, "head", to_near)
    from_side = lax.ppermute(n_side, "head", to_side)
    begun_l, begun_r = begin(n_near, n_side, out_weight)
    w_l, w_r = gather(pick, (whole_l, mine_l, theirs_l), (whole_r, mine_r, theirs_r))
    keep_l, send_l = pass_on(begun_l, from_near, w_l, "left")
    swap_l = lax.ppermute(send_l, "head", swap)
    keep_r, send_r = pass_on(begun_r, from_side, w_r, "right")
    swap_r = lax.ppermute(send_r, "head", swap)
    both_l = join(keep_l, swap_l, "join_left")
    both_r = join(keep_r, swap_r, "join_right")
    far_l = lax.ppermute(both_l, "head", to_side)
    far_r = lax.ppermute(both_r, "head", to_near)
    n_own, _, _ = lax.optimization_barrier((n_own, both_l, both_r))
    keep, *sends = own_part(n_own, out_weight, (from_near, from_side), (w_l, w_r))
    swaps = [lax.ppermute(send, "head", swap) for send in sends]
    return finish(keep, far_l, far_r, swaps)


def solution(mesh):
    return jax.shard_map(
        body,
        mesh=mesh,
        in_specs=(
            P("seq", "head", None),
            P("seq", "head", None),
            P("seq", "head", None),
            P("seq", "head"),
            P("seq", "head", None),
            P("head", None),
            P("head", None),
        ),
        out_specs=P(("seq", "head"), None),
        check_vma=False,
    )
```
